256 devices in a mesh: dp: 4 (over x), fsdp: 64 (over z, y, core).
Axes of the slice: x: 4, y: 4, z: 8, core: 2. Of those that a mesh axis runs over, the one named last changes fastest.
Arguments:
- inputs: bfloat16 [512, 16384], P('dp', 'fsdp'), may hold values from -140 to 140
- norm_gain_vector: bfloat16 [16384], P('fsdp'), may hold values from 0.5 to 1.5
- weight: bfloat16 [16384, 16384], P(None, 'fsdp'), may hold values from -0.046875 to 0.046875
- down_adapters: bfloat16 [16384, 16, 32], P('fsdp'), may hold values from -0.046875 to 0.046875
- up_adapters: bfloat16 [16, 32, 16384], P(None, None, 'fsdp'), may hold values from -1 to 1
- tenant: int32 [512], P('dp'), may hold values from 0 to 15
- tenant_slot_index: int32 [16], replicated, may hold values from 0 to 31, as said below
- live_row_count: int32 [4], P('dp'), may hold values from 1 to 128, 320 in all
- cotangent: bfloat16 [512, 16384], P('dp', 'fsdp'), may hold values from -6 to 6
- down_row_factor: float32 [32, 16384], P('dp', 'fsdp'), may hold values from 300 to 30000
- down_column_factor: float32 [32, 32], P('dp'), may hold values from 300 to 30000
- up_row_factor: float32 [32, 32], P('dp'), may hold values from 0.5 to 50
- up_column_factor: float32 [32, 16384], P('dp', 'fsdp'), may hold values from 0.5 to 50
Outputs:
- projected: bfloat16 [512, 16384], P('dp', 'fsdp')
- normed_gradient_transposed: bfloat16 [16384, 512], P('fsdp', 'dp')
- update_a: float32 [32, 16384, 32], P('dp', 'fsdp')
- update_b: float32 [32, 32, 16384], P('dp', None, 'fsdp')
- row_a_new: float32 [32, 16384], P('dp', 'fsdp')
- col_a_new: float32 [32, 32], P('dp')
- row_b_new: float32 [32, 32], P('dp')
- col_b_new: float32 [32, 16384], P('dp', 'fsdp')
The draws below stay inside these ranges and needn't reach their ends.
Inputs may be any that keep to these rules, and one draw needn't show every extreme that they name: Distinct slots; tenant t's optimizer state is in slot tenant_slot_index[t], owned by data group tenant_slot_index[t] // 8; every group owns at most 8 tenants and some group owns exactly 8. The first live_row_count[g] rows of data group g are live; some group has all 128 live; the counts sum to 320.
All inputs are finite; a program needn't handle non-finite values.
Results may differ from the reference program's by a relative error of at most 0.0095.
Values may be sent and summed in bfloat16 or wider, within the bound.
No kernel may reach another device: no remote copies, remote signals or barrier semaphores. Data moves between devices by JAX's collectives and lax.ppermute only.
A program may use at most 128 MiB of HBM per device.

```python
import math
import jax
import jax.numpy as jnp
import numpy as np
from jax import lax

MODEL_WIDTH = 16384
ADAPTER_RANK = 32
TENANT_COUNT = 16
CAP = 8
ROWS = 128
ROWS_ALL = 512
SLOTS = 32
N_DP = 4


def draw_inputs(key, part):
    key_base, key_cols, key_rows = jax.random.split(jax.random.fold_in(key, 11), 3)
    position = jnp.arange(MODEL_WIDTH, dtype=jnp.float32) / MODEL_WIDTH
    columns = jnp.exp(jnp.log(3.0) * position) * jnp.exp(jax.random.uniform(key_cols, (MODEL_WIDTH,), jnp.float32, 0.0, 1.2))
    rowscale = jnp.exp(jax.random.uniform(key_rows, (ROWS_ALL, 1), jnp.float32, 0.0, jnp.log(10.0)))
    frozen_output = jnp.clip(jax.random.normal(key_base, (ROWS_ALL, MODEL_WIDTH), jnp.float32), -4.0, 4.0)
    return (frozen_output * columns[None, :] * rowscale / 3.0).astype(jnp.bfloat16)


def draw_tenant_slot_index(key, part):
    key_full, key_order, key_other = jax.random.split(jax.random.fold_in(key, 23), 3)
    full = jax.random.randint(key_full, (), 0, N_DP)
    order = jax.random.permutation(key_order, TENANT_COUNT)
    others = jax.random.permutation(key_other, (N_DP - 1) * CAP)
    group = others // CAP
    group = group + (group >= full).astype(jnp.int32)
    other_slots = (group * CAP + others % CAP).astype(jnp.int32)
    filler = jnp.concatenate([jnp.zeros((CAP,), jnp.int32), other_slots[:TENANT_COUNT - CAP]])
    ranked = jnp.arange(TENANT_COUNT, dtype=jnp.int32)
    slot_by_rank = jnp.where(ranked < CAP, full * CAP + ranked, filler).astype(jnp.int32)
    return jnp.zeros((TENANT_COUNT,), jnp.int32).at[order].set(slot_by_rank)


def set_ends(result, stream_key, low, largest):
    longest = result.shape.index(max(result.shape))
    spots = []
    for shift in (0, 1):
        where = [jax.random.randint(jax.random.fold_in(stream_key, axis), (), 0, length) for axis, length in enumerate(result.shape)]
        where[longest] = (where[longest] + shift) % result.shape[longest]
        spots.append(tuple(where))
    return result.at[spots[0]].set(low).at[spots[1]].set(largest)


def block_scale(stream_key, dims, cuts, smallest, largest):
    factor_of, own = 1.0, jax.random.fold_in(stream_key, 6)
    for axis_at, blocks in cuts:
        steps = jnp.exp(jax.random.uniform(jax.random.fold_in(own, axis_at), (blocks,), jnp.float32, smallest / len(cuts), largest / len(cuts)))
        factor_of = factor_of * jnp.repeat(steps, dims[axis_at] // blocks).reshape([-1 if axis == axis_at else 1 for axis in range(len(dims))])
    return factor_of


def cumulative_ranks(count, lean):
    loads = [(1 << 20) // math.isqrt(rank ** lean) + 1 for rank in range(1, count + 1)]
    width = 1 + sum(loads) // (1 << 30)
    return np.cumsum(np.array([max(1, weight // width) for weight in loads]))


def skewed_ids(stream_key, dims, number_of, lean):
    table = cumulative_ranks(number_of, lean)
    ticket = jax.random.randint(jax.random.fold_in(stream_key, 1), dims, 0, int(table[number_of - 1]))
    rank = jnp.searchsorted(jnp.asarray(table, jnp.int32), ticket, side="right")
    return jax.random.permutation(jax.random.fold_in(stream_key, 2), number_of)[rank].astype(jnp.int32)


def split_up(number_of, total, most, lean):
    loads = [(1 << 20) // math.isqrt(standing ** lean) + 1 for standing in range(2, number_of + 1)]
    spare, counts = total - most - (number_of - 1), [1] * (number_of - 1)
    while spare > 0:
        candidates = [i for i in range(number_of - 1) if counts[i] < most]
        pool, budget = sum([loads[i] for i in candidates]), spare
        for i in candidates:
            addition = min(most - counts[i], max(1, budget * loads[i] // pool), spare)
            counts[i] = counts[i] + addition
            spare = spare - addition
    return np.array([most] + counts)


def uneven(rng, number_of, total, bound, slope):
    if number_of == 2:
        one = jax.random.randint(rng, (), max(1, total - bound), min(bound, total - 1) + 1)
        return jnp.stack([one, total - one])
    lengths = jnp.asarray(split_up(number_of, total, bound, slope), jnp.int32)
    couples = (number_of - 1) // 2
    giver, taker = lengths[1:1 + 2 * couples:2], lengths[2:2 + 2 * couples:2]
    margin = jnp.minimum(giver - 1, bound - taker)
    shifted = jax.random.randint(jax.random.fold_in(rng, 1), (couples,), 0, 1 << 20) % (margin + 1)
    lengths = lengths.at[1:1 + 2 * couples:2].set(giver - shifted).at[2:2 + 2 * couples:2].set(taker + shifted)
    return lengths[jax.random.permutation(jax.random.fold_in(rng, 2), number_of)]


def gaussian(stream_key, shape, deviation, most, shards=(), kind=jnp.bfloat16):
    values = deviation * jax.random.normal(stream_key, shape, jnp.float32)
    if shards:
        values = values * block_scale(stream_key, shape, shards, -0.22, 0.18)
    return jnp.clip(values, -most, most).astype(kind)


def setup_inputs(seed: int = 0) -> dict:
    splits = jax.random.split(jax.random.key(seed), 14)
    inputs = draw_inputs(jax.random.fold_in(splits[13], 71), 0)
    norm_gain_vector = jnp.clip(1.0 + 0.1 * jax.random.normal(splits[1], (MODEL_WIDTH,), jnp.float32), 0.5, 1.5).astype(jnp.bfloat16)
    weight = gaussian(splits[2], (MODEL_WIDTH, MODEL_WIDTH), MODEL_WIDTH ** -0.5, 0.046875, ((1, 64),))
    down_adapters = gaussian(splits[3], (MODEL_WIDTH, TENANT_COUNT, ADAPTER_RANK), MODEL_WIDTH ** -0.5, 0.046875, ((0, 64),))
    up_adapters = gaussian(splits[4], (TENANT_COUNT, ADAPTER_RANK, MODEL_WIDTH), ADAPTER_RANK ** -0.5, 1.0, ((2, 64),))
    tenant = set_ends(skewed_ids(splits[5], (ROWS_ALL,), TENANT_COUNT, 2), jax.random.fold_in(splits[5], 3), 0, TENANT_COUNT - 1).astype(jnp.int32)
    tenant_slot_index = draw_tenant_slot_index(jax.random.fold_in(splits[13], 71), 0)
    live_row_count = uneven(splits[7], N_DP, (N_DP + 1) * ROWS // 2, ROWS, 0).astype(jnp.int32)
    cotangent = gaussian(splits[8], (ROWS_ALL, MODEL_WIDTH), 1.0, 6.0, ((0, 4), (1, 64)))
    down_row_factor = jnp.clip(jnp.exp(math.log(30000.0) - 4.6051702 * jax.random.uniform(splits[9], (SLOTS, MODEL_WIDTH), jnp.float32) ** block_scale(splits[9], (SLOTS, MODEL_WIDTH), ((0, 4), (1, 64)), -0.2, 0.2)), 300.0, 30000.0)
    down_column_factor = jnp.clip(jnp.exp(math.log(30000.0) - 4.6051702 * jax.random.uniform(splits[10], (SLOTS, ADAPTER_RANK), jnp.float32) ** block_scale(splits[10], (SLOTS, ADAPTER_RANK), ((0, 4),), -0.2, 0.2)), 300.0, 30000.0)
    up_row_factor = jnp.clip(jnp.exp(math.log(50.0) - 4.6051702 * jax.random.uniform(splits[11], (SLOTS, ADAPTER_RANK), jnp.float32) ** block_scale(splits[11], (SLOTS, ADAPTER_RANK), ((0, 4),), -0.2, 0.2)), 0.5, 50.0)
    up_column_factor = jnp.clip(jnp.exp(math.log(50.0) - 4.6051702 * jax.random.uniform(splits[12], (SLOTS, MODEL_WIDTH), jnp.float32) ** block_scale(splits[12], (SLOTS, MODEL_WIDTH), ((0, 4), (1, 64)), -0.2, 0.2)), 0.5, 50.0)
    return dict(inputs=inputs, norm_gain_vector=norm_gain_vector, weight=weight, down_adapters=down_adapters, up_adapters=up_adapters, tenant=tenant, tenant_slot_index=tenant_slot_index, live_row_count=live_row_count, cotangent=cotangent, down_row_factor=down_row_factor, down_column_factor=down_column_factor, up_row_factor=up_row_factor, up_column_factor=up_column_factor)


ADAPTER_SCALE = 0.5
BETA_TWO = 0.9
SQ_EPS = 1e-30
RMS_EPS = 1e-05

def reference(inputs, norm_gain_vector, weight, down_adapters, up_adapters, tenant, tenant_slot_index, live_row_count, cotangent, down_row_factor, down_column_factor, up_row_factor, up_column_factor):
    highest_precision = lax.Precision.HIGHEST
    xf = inputs.astype(jnp.float32)
    power = lax.optimization_barrier(jnp.sum(xf * xf, axis=1, keepdims=True))
    scale = lax.rsqrt(power / MODEL_WIDTH + RMS_EPS)
    normalized_input = (xf * scale * norm_gain_vector.astype(jnp.float32)).astype(jnp.bfloat16)
    pick = tenant[:, None] == jnp.arange(TENANT_COUNT, dtype=jnp.int32)[None, :]
    pick_b = pick.astype(jnp.bfloat16)
    pick_f = pick.astype(jnp.float32)
    down_flattened = down_adapters.reshape(MODEL_WIDTH, TENANT_COUNT * ADAPTER_RANK)
    up_flattened = up_adapters.reshape(TENANT_COUNT * ADAPTER_RANK, MODEL_WIDTH)
    inner_all = jnp.dot(normalized_input, down_flattened, preferred_element_type=jnp.float32)
    inner = lax.optimization_barrier(jnp.sum(inner_all.reshape(ROWS_ALL, TENANT_COUNT, ADAPTER_RANK) * pick_f[:, :, None], axis=1))
    spread_rows = (inner.astype(jnp.bfloat16)[:, None, :] * pick_b[:, :, None]).reshape(ROWS_ALL, TENANT_COUNT * ADAPTER_RANK)
    frozen_output = jnp.dot(normalized_input, weight, preferred_element_type=jnp.float32)
    adapted_output = jnp.dot(spread_rows, up_flattened, preferred_element_type=jnp.float32)
    projected = (frozen_output + ADAPTER_SCALE * adapted_output).astype(jnp.bfloat16)
    index = jnp.arange(ROWS_ALL, dtype=jnp.int32)
    live = index % ROWS < live_row_count[index // ROWS]
    output_gradient = jnp.where(live[:, None], cotangent, jnp.zeros_like(cotangent))
    back_all = jnp.dot(output_gradient, up_flattened.T, preferred_element_type=jnp.float32)
    back = lax.optimization_barrier(jnp.sum(back_all.reshape(ROWS_ALL, TENANT_COUNT, ADAPTER_RANK) * pick_f[:, :, None], axis=1))
    backward_spread_rows = (back.astype(jnp.bfloat16)[:, None, :] * pick_b[:, :, None]).reshape(ROWS_ALL, TENANT_COUNT * ADAPTER_RANK)
    frozen_input_gradient = jnp.dot(weight, output_gradient.T, preferred_element_type=jnp.float32)
    adapter_input_gradient = jnp.dot(down_flattened, backward_spread_rows.T, preferred_element_type=jnp.float32)
    normed_gradient_transposed = (frozen_input_gradient + ADAPTER_SCALE * adapter_input_gradient).astype(jnp.bfloat16)
    down_gradient = (ADAPTER_SCALE * jnp.dot(normalized_input.T, backward_spread_rows, preferred_element_type=jnp.float32)).reshape(MODEL_WIDTH, TENANT_COUNT, ADAPTER_RANK)
    up_gradient = (ADAPTER_SCALE * jnp.dot(spread_rows.T, output_gradient, preferred_element_type=jnp.float32)).reshape(TENANT_COUNT, ADAPTER_RANK, MODEL_WIDTH)
    owner_routing = (tenant_slot_index[None, :] == jnp.arange(SLOTS, dtype=jnp.int32)[:, None]).astype(jnp.float32)
    ga = jnp.einsum('st,dtr->sdr', owner_routing, down_gradient, precision=highest_precision)
    gb = jnp.einsum('st,trd->srd', owner_routing, up_gradient, precision=highest_precision)
    sq_a = ga * ga + SQ_EPS
    sq_b = gb * gb + SQ_EPS
    row_a_new = BETA_TWO * down_row_factor + (1.0 - BETA_TWO) * (lax.optimization_barrier(jnp.sum(sq_a, axis=2)) / ADAPTER_RANK)
    col_a_new = BETA_TWO * down_column_factor + (1.0 - BETA_TWO) * (lax.optimization_barrier(jnp.sum(sq_a, axis=1)) / MODEL_WIDTH)
    row_b_new = BETA_TWO * up_row_factor + (1.0 - BETA_TWO) * (lax.optimization_barrier(jnp.sum(sq_b, axis=2)) / MODEL_WIDTH)
    col_b_new = BETA_TWO * up_column_factor + (1.0 - BETA_TWO) * (lax.optimization_barrier(jnp.sum(sq_b, axis=1)) / ADAPTER_RANK)
    mean_a = lax.optimization_barrier(jnp.sum(row_a_new, axis=1)) / MODEL_WIDTH
    mean_b = lax.optimization_barrier(jnp.sum(row_b_new, axis=1)) / ADAPTER_RANK
    update_a = ga * lax.rsqrt(row_a_new[:, :, None] * col_a_new[:, None, :] / mean_a[:, None, None])
    update_b = gb * lax.rsqrt(row_b_new[:, :, None] * col_b_new[:, None, :] / mean_b[:, None, None])
    return (projected, normed_gradient_transposed, update_a, update_b, row_a_new, col_a_new, row_b_new, col_b_new)
```

```python
import jax
import jax.numpy as jnp
from jax import lax
from jax.sharding import Mesh, PartitionSpec as P

ADAPTER_SCALE = 0.5
BETA_TWO = 0.9
SQ_EPS = 1e-30
RMS_EPS = 1e-05
NX, NZ, NY, NC = 4, 8, 4, 2
F = ("z", "y", "core")
bf16, f32 = jnp.bfloat16, jnp.float32
LAST = (((1,), (1,)), ((), ()))
FIRST = (((0,), (0,)), ((), ()))


def plane_moves(rule):
    pairs = []
    for z in range(NZ):
        for y in range(NY):
            for c in range(NC):
                to = rule(z, y, c)
                if to is not None:
                    z2, y2, c2 = to
                    pairs.append(
                        ((z * NY + y) * NC + c, ((z2 % NZ) * NY + y2 % NY) * NC + c2)
                    )
    return pairs


Z_BY_CORE = plane_moves(lambda z, y, c: (z + 1 - 2 * c, y, c))
Y_BY_CORE = plane_moves(lambda z, y, c: (z, y + 1 - 2 * c, c))


def turn(n, k):
    return [(i, (i + k) % n) for i in range(n)]


def swap(v):
    return lax.ppermute(v, "core", turn(NC, 1))


def all_sum(v, core):
    v = v + swap(v)
    a = lax.ppermute(v, F, plane_moves(lambda z, y, c: (z, y ^ (1 + c), c)))
    b = lax.ppermute(v, F, plane_moves(lambda z, y, c: (z, y ^ 3, c) if c else None))
    q = jnp.where(core == 0, v + a, a + b)
    v = q + swap(q)
    a, b, d = [
        lax.ppermute(v, F, plane_moves(lambda z, y, c: (z ^ (k + 3 * c), y, c)))
        for k in (1, 2, 3)
    ]
    e = lax.ppermute(v, F, plane_moves(lambda z, y, c: (z ^ 7, y, c) if c else None))
    q = jnp.where(core == 0, (v + a) + (b + d), (a + b) + (d + e))
    return q + swap(q)


def dot(a, b, dims):
    return lax.dot_general(a, b, dims, preferred_element_type=f32)


def on_device(
    inputs,
    norm_gain_vector,
    weight,
    down_adapters,
    up_adapters,
    tenant,
    tenant_slot_index,
    live_row_count,
    cotangent,
    down_row_factor,
    down_column_factor,
    up_row_factor,
    up_column_factor,
):
    rows, width = inputs.shape
    full_width = weight.shape[0]
    tenants, rank = down_adapters.shape[1:]
    owned = down_row_factor.shape[0]
    z, y, core = lax.axis_index("z"), lax.axis_index("y"), lax.axis_index("core")
    opposite = 1 - core
    sign = 1 - 2 * core

    x_f = inputs.astype(f32)
    gained = (x_f * norm_gain_vector.astype(f32)).astype(bf16)
    power = jnp.sum(x_f * x_f, axis=1)
    live = lax.iota(jnp.int32, rows) < live_row_count[0]
    grad_out = jnp.where(live[:, None], cotangent, jnp.zeros_like(cotangent))

    both = jnp.stack([gained, grad_out])
    both_all = [both] + [lax.ppermute(both, "dp", turn(NX, k)) for k in (1, 3, 2)]

    down_flat = down_adapters.reshape(width, tenants * rank)
    up_flat = up_adapters.reshape(tenants * rank, width)
    pick = (lax.iota(jnp.int32, tenants)[:, None] == tenant[None, :])[:, None, :]
    inner_part = jnp.sum(
        dot(down_flat, gained, (((0,), (1,)), ((), ()))).reshape(tenants, rank, rows)
        * pick.astype(f32),
        axis=0,
    )
    back_part = jnp.sum(
        dot(up_flat, grad_out, LAST).reshape(tenants, rank, rows) * pick.astype(f32), axis=0
    )
    packed = jnp.concatenate(
        [inner_part, back_part, jnp.broadcast_to(power[None, :], (8, rows))], axis=0
    )
    total = all_sum(packed, core)
    scale = lax.rsqrt(total[2 * rank] / full_width + RMS_EPS)
    inner = (total[:rank] * scale[None, :]).astype(bf16)
    back = total[rank : 2 * rank]
    back_b = back.astype(bf16)
    small = jnp.concatenate(
        [
            inner,
            (back * scale[None, :]).astype(bf16),
            jnp.broadcast_to(tenant.astype(bf16)[None, :], (16, rows)),
        ],
        axis=0,
    )
    small_all = [small] + [lax.ppermute(small, "dp", turn(NX, k)) for k in (1, 3, 2)]

    w_by = weight.reshape(NZ, NY, NC, width, width)

    def part(at_y, at_c):
        rows_of = lax.dynamic_slice(
            w_by, (0, at_y % NY, at_c, 0, 0), (NZ, 1, 1, width, width)
        ).reshape(NZ * width, width)
        return dot(rows_of, grad_out, LAST)

    keep_y, send_y = y + 1 + 2 * core, y + 3 + 2 * core
    r_two = swap(part(y + 2, opposite).astype(bf16))
    r_far = swap(part(send_y, core).astype(bf16))
    r_near = swap(part(send_y, opposite).astype(bf16))
    r_own = swap(part(y, opposite).astype(bf16))
    t_two = (part(y + 2, core) + r_two).astype(bf16)
    g_two = lax.ppermute(t_two, F, Y_BY_CORE)
    t_far = (part(keep_y, opposite) + r_far).astype(bf16)
    g_far = lax.ppermute(t_far, F, Y_BY_CORE)
    t_near = (part(keep_y, core) + r_near + g_two).astype(bf16)
    g_near = lax.ppermute(t_near, F, Y_BY_CORE)
    g_other = swap(g_far)
    reduced = (part(y, core) + r_own + g_other + g_near).astype(bf16)
    reduced = reduced.reshape(NZ, width, rows)

    def of_z(k):
        return lax.dynamic_index_in_dim(reduced, (z + k) % NZ, 0, keepdims=False)

    pieces = [
        lax.ppermute(of_z(k), "z", turn(NZ, k)).astype(f32) for k in (4, 3, 5, 2, 6, 1, 7)
    ]
    frozen_gradient = of_z(0).astype(f32)
    for piece in pieces:
        frozen_gradient = frozen_gradient + piece

    over_y = [gained] + [lax.ppermute(gained, "y", turn(NY, k)) for k in (3, 2, 1)]
    own_y = lax.dynamic_slice_in_dim(jnp.stack(over_y + over_y), (NY - y) % NY, NY, 0)
    other_y = swap(own_y)
    block = jnp.stack(
        [jnp.where(core == 0, own_y, other_y), jnp.where(core == 0, other_y, own_y)], axis=1
    ).reshape(2, NY // 2 * NC, rows, width)
    w_half = weight.reshape(NZ * 2, NY // 2 * NC, width, width)

    def times(x, at_z, half):
        w = lax.dynamic_index_in_dim(w_half, (at_z % NZ) * 2 + half, 0, keepdims=False)
        return dot(x, w, (((0, 2), (0, 1)), ((), ())))

    first, second = block[0], block[1]
    frozen = times(first, z, 0) + times(second, z, 1)
    for s in (1, 2, 3):
        first = lax.ppermute(first, F, Z_BY_CORE)
        second = lax.ppermute(second, F, Z_BY_CORE)
        first_o, second_o = swap(first), swap(second)
        frozen = frozen + times(first, z + NZ - s * sign, 0)
        frozen = frozen + times(second, z + NZ - s * sign, 1)
        frozen = frozen + times(first_o, z + NZ + s * sign, 0)
        frozen = frozen + times(second_o, z + NZ + s * sign, 1)
    final = lax.ppermute(jnp.where(core == 0, first, second), F, Z_BY_CORE)
    final_o = swap(final)
    frozen = frozen + times(final, z + NZ // 2, core)
    frozen = frozen + times(final_o, z + NZ // 2, opposite)

    pick_b = pick.astype(bf16)
    spread = (inner[None] * pick_b).reshape(tenants * rank, rows)
    back_spread = (back_b[None] * pick_b).reshape(tenants * rank, rows)
    projected = (
        scale[:, None] * frozen + ADAPTER_SCALE * dot(spread, up_flat, FIRST)
    ).astype(bf16)
    adapter_gradient = jnp.dot(down_flat, back_spread, preferred_element_type=f32)
    normed_gradient_transposed = (frozen_gradient + ADAPTER_SCALE * adapter_gradient).astype(bf16)

    mine = lax.iota(jnp.int32, owned) + lax.axis_index("dp") * owned
    routes = (tenant_slot_index[None, :] == mine[:, None]).astype(bf16)
    small_all = jnp.concatenate(small_all, axis=1)
    x_all = jnp.concatenate([b[0] for b in both_all])
    g_all = jnp.concatenate([b[1] for b in both_all])
    tenant_all = small_all[2 * rank]
    pick_all = (lax.iota(jnp.int32, tenants).astype(bf16)[:, None] == tenant_all[None, :]).astype(
        bf16
    )
    slot_rows = jnp.dot(routes, pick_all, preferred_element_type=f32).astype(bf16)[:, None, :]
    all_rows = NX * rows
    a_rows = (small_all[None, rank : 2 * rank] * slot_rows).reshape(owned * rank, all_rows)
    b_rows = (small_all[None, :rank] * slot_rows).reshape(owned * rank, all_rows)
    ga = (ADAPTER_SCALE * jnp.dot(a_rows, x_all, preferred_element_type=f32)).reshape(
        owned, rank, width
    )
    gb = (ADAPTER_SCALE * jnp.dot(b_rows, g_all, preferred_element_type=f32)).reshape(
        owned, rank, width
    )
    sq_a = ga * ga + SQ_EPS
    sq_b = gb * gb + SQ_EPS
    row_a_new = BETA_TWO * down_row_factor + (1.0 - BETA_TWO) * (jnp.sum(sq_a, axis=1) / rank)
    col_b_new = BETA_TWO * up_column_factor + (1.0 - BETA_TWO) * (jnp.sum(sq_b, axis=1) / rank)
    moments = jnp.concatenate(
        [
            jnp.sum(sq_a, axis=2),
            jnp.sum(sq_b, axis=2),
            jnp.broadcast_to(jnp.sum(row_a_new, axis=1, keepdims=True), (owned, 2 * rank)),
        ],
        axis=1,
    )
    moments = all_sum(moments, core)
    col_a_new = BETA_TWO * down_column_factor + (1.0 - BETA_TWO) * (
        moments[:, :rank] / full_width
    )
    row_b_new = BETA_TWO * up_row_factor + (1.0 - BETA_TWO) * (
        moments[:, rank : 2 * rank] / full_width
    )
    mean_a = moments[:, 2 * rank] / full_width
    mean_b = jnp.sum(row_b_new, axis=1) / rank
    update_a = ga * lax.rsqrt(row_a_new[:, None, :] * col_a_new[:, :, None] / mean_a[:, None, None])
    update_b = gb * lax.rsqrt(row_b_new[:, :, None] * col_b_new[:, None, :] / mean_b[:, None, None])
    return (
        projected,
        normed_gradient_transposed,
        jnp.swapaxes(update_a, 1, 2),
        update_b,
        row_a_new,
        col_a_new,
        row_b_new,
        col_b_new,
    )


def solution(mesh):
    split = Mesh(mesh.devices.reshape(NX, NZ, NY, NC), ("dp",) + F)
    return jax.shard_map(
        on_device,
        mesh=split,
        in_specs=(
            P("dp", F),
            P(F),
            P(None, F),
            P(F, None, None),
            P(None, None, F),
            P("dp"),
            P(),
            P("dp"),
            P("dp", F),
            P("dp", F),
            P("dp", None),
            P("dp", None),
            P("dp", F),
        ),
        out_specs=(
            P("dp", F),
            P(F, "dp"),
            P("dp", F, None),
            P("dp", None, F),
            P("dp", F),
            P("dp", None),
            P("dp", None),
            P("dp", F),
        ),
        check_vma=False,
    )
```

```python
import functools

import jax
import jax.numpy as jnp
from jax import lax
from jax.experimental import pallas as pl
from jax.experimental.pallas import tpu as pltpu
from jax.sharding import Mesh, PartitionSpec as P

ADAPTER_SCALE = 0.5
BETA_TWO = 0.9
SQ_EPS = 1e-30
RMS_EPS = 1e-05
NX, NZ, NY, NC = 4, 8, 4, 2
F = ("z", "y", "core")
bf16, f32, i32 = jnp.bfloat16, jnp.float32, jnp.int32
NT = (((1,), (1,)), ((), ()))
NN = (((1,), (0,)), ((), ()))
TN = (((0,), (0,)), ((), ()))
ROWS, WIDTH, FULL, TENANTS, RANK, OWNED = 128, 256, 16384, 16, 32, 8
HBM = pl.BlockSpec(memory_space=pl.ANY)
VMEM = pl.BlockSpec(memory_space=pltpu.VMEM)
SMEM = pl.BlockSpec(memory_space=pltpu.SMEM)


def plane_moves(rule):
    pairs = []
    for z in range(NZ):
        for y in range(NY):
            for c in range(NC):
                to = rule(z, y, c)
                if to is not None:
                    z2, y2, c2 = to
                    pairs.append(
                        ((z * NY + y) * NC + c, ((z2 % NZ) * NY + y2 % NY) * NC + c2)
                    )
    return pairs


Z_BY_CORE = plane_moves(lambda z, y, c: (z + 1 - 2 * c, y, c))
Y_BY_CORE = plane_moves(lambda z, y, c: (z, y + 1 - 2 * c, c))


def turn(n, k):
    return [(i, (i + k) % n) for i in range(n)]


def swap(v):
    return lax.ppermute(v, "core", turn(NC, 1))


def like(shape, dtype):
    return jax.ShapeDtypeStruct(shape, dtype)


def params(n=48):
    return pltpu.CompilerParams(vmem_limit_bytes=n * 1024 * 1024)


def cost(flops, moved):
    return pl.CostEstimate(flops=flops, bytes_accessed=moved, transcendentals=0)


def dot(a, b, dims=NN):
    return lax.dot_general(a, b, dims, preferred_element_type=f32)


def column_to_rows(v):
    return jnp.broadcast_to(v, (v.shape[0], 128)).T


def row_to_columns(v):
    return jnp.broadcast_to(v, (128, v.shape[1])).T


def rows_body(live_ref, x_ref, gain_ref, cot_ref, gained_ref, grad_ref, turned_ref):
    gained_ref[...] = (x_ref[...].astype(f32) * gain_ref[...].astype(f32)).astype(bf16)
    at = lax.broadcasted_iota(i32, (ROWS, WIDTH), 0)
    grad = jnp.where(at < live_ref[0], cot_ref[...].astype(f32), 0.0)
    grad_ref[...] = grad.astype(bf16)
    turned_ref[...] = grad.T.astype(bf16)


def rows_kernel(live, x, gain, cot):
    return pl.pallas_call(
        rows_body,
        in_specs=[SMEM, VMEM, VMEM, VMEM],
        out_specs=[VMEM] * 3,
        out_shape=[like((ROWS, WIDTH), bf16)] * 2 + [like((WIDTH, ROWS), bf16)],
        compiler_params=params(),
    )(live, x, gain, cot)


def inner_body(x_ref, gained_ref, grad_ref, down_ref, up_ref, tenant_ref, out_ref):
    tenant = tenant_ref[...]
    for at, w_ref, v_ref in ((0, down_ref, gained_ref), (RANK, up_ref, grad_ref)):
        every = dot(w_ref[...], v_ref[...], NT)
        picked = jnp.zeros((RANK, ROWS), f32)
        for t in range(TENANTS):
            picked = picked + jnp.where(tenant == t, every[t * RANK : (t + 1) * RANK], 0.0)
        out_ref[at : at + RANK] = picked
    x = x_ref[...].astype(f32)
    out_ref[2 * RANK :] = column_to_rows(jnp.sum(x * x, axis=1, keepdims=True))[:8]


def inner_kernel(x, gained, grad, down, up, tenant):
    return pl.pallas_call(
        inner_body,
        in_specs=[VMEM] * 6,
        out_specs=VMEM,
        out_shape=like((2 * RANK + 8, ROWS), f32),
        compiler_params=params(),
        cost_estimate=cost(2**26, 2**20),
    )(x, gained, grad, down, up, tenant)


def part_body(counts, spots_ref, turned_ref, *refs):
    n = len(counts)
    refs = list(refs)
    w = [refs.pop(0) for _ in range(n)]
    adds = [[refs.pop(0) for _ in range(k)] for k in counts]
    outs = refs[len(refs) - n :]
    turned = turned_ref[...]
    for i in range(n):
        for at in range(w[i].shape[0]):
            total = dot(w[i][at, 0, 0], turned)
            for a in adds[i]:
                total = total + a[at].astype(f32)
            outs[i][at] = total.astype(bf16)


def part_kernel(w5, turned, spots, first, adds, tokens, tiles=4):
    n = len(adds)
    step = NZ // tiles
    w_specs = [
        pl.BlockSpec(
            (step, 1, 1, WIDTH, WIDTH),
            lambda i, s, k=k: (i, s[2 * (first + k)], s[2 * (first + k) + 1], 0, 0),
        )
        for k in range(n)
    ]
    tile = pl.BlockSpec((step, WIDTH, ROWS), lambda i, s: (i, 0, 0))
    flat = [a for some in adds for a in some]
    return pl.pallas_call(
        functools.partial(part_body, [len(a) for a in adds]),
        grid_spec=pltpu.PrefetchScalarGridSpec(
            num_scalar_prefetch=1,
            grid=(tiles,),
            in_specs=[pl.BlockSpec((WIDTH, ROWS), lambda i, s: (0, 0))]
            + w_specs
            + [tile] * len(flat)
            + [HBM] * len(tokens),
            out_specs=[tile] * n,
        ),
        out_shape=[like((NZ, WIDTH, ROWS), bf16)] * n,
        compiler_params=params(),
        cost_estimate=cost(n * 2**27, n * 2**21),
    )(spots, turned, *([w5] * n), *flat, *tokens)


def last_part_body(spots_ref, turned_ref, w_ref, a_ref, b_ref, c_ref, *refs):
    outs = refs[len(refs) - NZ :]
    turned = turned_ref[...]
    z = spots_ref[16]
    for k in range(NZ):
        at = (z + k) % NZ
        total = dot(w_ref[at, 0, 0], turned)
        for a in (a_ref, b_ref, c_ref):
            total = total + a[at].astype(f32)
        outs[k][...] = total.astype(bf16)


def last_part_kernel(w5, turned, spots, at, adds, tokens):
    whole = pl.BlockSpec((NZ, WIDTH, ROWS), lambda i, s: (0, 0, 0))
    flat = pl.BlockSpec((WIDTH, ROWS), lambda i, s: (0, 0))
    return pl.pallas_call(
        last_part_body,
        grid_spec=pltpu.PrefetchScalarGridSpec(
            num_scalar_prefetch=1,
            grid=(1,),
            in_specs=[
                flat,
                pl.BlockSpec(
                    (NZ, 1, 1, WIDTH, WIDTH), lambda i, s: (0, s[2 * at], s[2 * at + 1], 0, 0)
                ),
            ]
            + [whole] * 3
            + [HBM] * len(tokens),
            out_specs=[flat] * NZ,
        ),
        out_shape=[like((WIDTH, ROWS), bf16)] * NZ,
        compiler_params=params(),
        cost_estimate=cost(2**27, 2**21),
    )(spots, turned, w5, *adds, *tokens)


def block_body(spots_ref, *refs):
    own, other, grad_ref = refs[:NY], refs[NY : 2 * NY], refs[2 * NY]
    block_ref, both_ref = refs[2 * NY + 1 :]
    y, core = spots_ref[17], spots_ref[18]
    for j in range(NY):
        at = ((y + j) % NY) * NC
        block_ref[at + core] = own[j][...]
        block_ref[at + 1 - core] = other[j][...]
    both_ref[0] = own[0][...]
    both_ref[1] = grad_ref[...]


def block_kernel(spots, own, other, grad):
    return pl.pallas_call(
        block_body,
        in_specs=[SMEM] + [VMEM] * (2 * NY + 1),
        out_specs=[VMEM] * 2,
        out_shape=[like((NY * NC, ROWS, WIDTH), bf16), like((2, ROWS, WIDTH), bf16)],
        compiler_params=params(),
    )(spots, *own, *other, grad)


def frozen_body(n, has_acc, spots_ref, *refs):
    refs = list(refs)
    acc_ref = refs.pop(0) if has_acc else None
    xs, ws, out_ref = refs[:n], refs[n : 2 * n], refs[2 * n]
    total = None
    for x_ref, w_ref in zip(xs, ws):
        for g in range(x_ref.shape[0]):
            term = dot(x_ref[g], w_ref[0, g])
            total = term if total is None else total + term

    @pl.when(pl.program_id(0) == 0)
    def _():
        out_ref[...] = total + acc_ref[...] if has_acc else total

    @pl.when(pl.program_id(0) > 0)
    def _():
        out_ref[...] = out_ref[...] + total


def frozen_kernel(w4, spots, acc, blocks, ats, tiles=4):
    n = len(blocks)
    flat = pl.BlockSpec((ROWS, WIDTH), lambda i, s: (0, 0))
    step = blocks[0].shape[0] // tiles
    has_acc = acc is not None
    return pl.pallas_call(
        functools.partial(frozen_body, n, has_acc),
        grid_spec=pltpu.PrefetchScalarGridSpec(
            num_scalar_prefetch=1,
            grid=(tiles,),
            in_specs=[flat] * has_acc
            + [pl.BlockSpec((step, ROWS, WIDTH), lambda i, s: (i, 0, 0))] * n
            + [
                pl.BlockSpec((1, step, WIDTH, WIDTH), lambda i, s, a=a: (s[a], i, 0, 0))
                for a in ats
            ],
            out_specs=flat,
        ),
        out_shape=like((ROWS, WIDTH), f32),
        compiler_params=params(),
        cost_estimate=cost(n * 2**27, n * 2**20),
    )(spots, *([acc] * has_acc), *blocks, *([w4] * n))


def final_body(spots_ref, acc_ref, a_ref, b_ref, wa_ref, wb_ref, scale_ref, small_ref, up_ref, tenant_ref, out_ref):
    total = acc_ref[...]
    for x_ref, w_ref in ((a_ref, wa_ref), (b_ref, wb_ref)):
        for g in range(x_ref.shape[0]):
            total = total + dot(x_ref[g], w_ref[0, g])
    tenant = tenant_ref[...]
    inner = small_ref[:RANK].astype(f32)
    spread = jnp.concatenate([jnp.where(tenant == t, inner, 0.0) for t in range(TENANTS)])
    adapted = dot(spread.T.astype(bf16), up_ref[...])
    scale = row_to_columns(scale_ref[:1])[:, :1]
    out_ref[...] = (scale * total + ADAPTER_SCALE * adapted).astype(bf16)


def final_kernel(w_half, spots, acc, a, b, scale, small, up, tenant):
    def full(v):
        return pl.BlockSpec(v.shape, lambda i, s, n=v.ndim: (0,) * n)

    half = (1, NY * NC // 2, WIDTH, WIDTH)
    return pl.pallas_call(
        final_body,
        grid_spec=pltpu.PrefetchScalarGridSpec(
            num_scalar_prefetch=1,
            grid=(1,),
            in_specs=[full(acc), full(a), full(b)]
            + [pl.BlockSpec(half, lambda i, s, k=k: (s[k], 0, 0, 0)) for k in (26, 27)]
            + [full(scale), full(small), full(up), full(tenant)],
            out_specs=full(acc),
        ),
        out_shape=like((ROWS, WIDTH), bf16),
        compiler_params=params(),
        cost_estimate=cost(2**28, 2**21),
    )(spots, acc, a, b, w_half, w_half, scale, small, up, tenant)


def gradient_body(*refs):
    pieces, (down_ref, back_ref, tenant_ref, out_ref) = refs[:NZ], refs[NZ:]
    total = pieces[0][...].astype(f32)
    for p in pieces[1:]:
        total = total + p[...].astype(f32)
    tenant = tenant_ref[...]
    back = back_ref[...].astype(f32)
    spread = jnp.concatenate([jnp.where(tenant == t, back, 0.0) for t in range(TENANTS)])
    adapter = dot(down_ref[...].astype(f32).T.astype(bf16), spread.astype(bf16))
    out_ref[...] = (total + ADAPTER_SCALE * adapter).astype(bf16)


def gradient_kernel(pieces, down, back, tenant):
    return pl.pallas_call(
        gradient_body,
        in_specs=[VMEM] * (NZ + 3),
        out_specs=VMEM,
        out_shape=like((WIDTH, ROWS), bf16),
        compiler_params=params(),
        cost_estimate=cost(2**25, 2**20),
    )(*pieces, down, back, tenant)


def small_body(a_ref, b_ref, tenant_ref, small_ref, back_ref, scale_ref):
    total = a_ref[...] + b_ref[...]
    scale = lax.rsqrt(total[2 * RANK : 2 * RANK + 1] / FULL + RMS_EPS)
    back = total[RANK : 2 * RANK]
    small_ref[:RANK] = (total[:RANK] * scale).astype(bf16)
    small_ref[RANK : 2 * RANK] = (back * scale).astype(bf16)
    small_ref[2 * RANK :] = jnp.broadcast_to(tenant_ref[...].astype(f32), (16, ROWS)).astype(bf16)
    back_ref[...] = back.astype(bf16)
    scale_ref[...] = jnp.broadcast_to(scale, (8, ROWS))


def small_kernel(a, b, tenant):
    return pl.pallas_call(
        small_body,
        in_specs=[VMEM] * 3,
        out_specs=[VMEM] * 3,
        out_shape=[
            like((2 * RANK + 16, ROWS), bf16),
            like((RANK, ROWS), bf16),
            like((8, ROWS), f32),
        ],
        compiler_params=params(),
    )(a, b, tenant)


def lift(v, size):
    return jnp.broadcast_to(v[:, None, :], (OWNED, RANK, size)).reshape(OWNED * RANK, size)


def slots_body(slot_ref, spots_ref, *refs):
    smalls, boths = refs[:NX], refs[NX : 2 * NX]
    row_ref, col_ref, ga_ref, gb_ref, row_out, col_out, sum_ref = refs[2 * NX :]
    first = spots_ref[19] * OWNED
    a_rows, b_rows = [], []
    for small_ref in smalls:
        tenant = small_ref[2 * RANK : 2 * RANK + 16].astype(f32)[:1]
        slot = jnp.full((1, ROWS), -1, i32)
        for t in range(TENANTS):
            slot = jnp.where(tenant == t, slot_ref[t], slot)
        inner = small_ref[:RANK].astype(f32)
        back = small_ref[RANK : 2 * RANK].astype(f32)
        a_rows.append(
            jnp.concatenate([jnp.where(slot == first + s, back, 0.0) for s in range(OWNED)])
        )
        b_rows.append(
            jnp.concatenate([jnp.where(slot == first + s, inner, 0.0) for s in range(OWNED)])
        )
    for rows, at, out_ref in ((a_rows, 0, ga_ref), (b_rows, 1, gb_ref)):
        total = dot(rows[0].astype(bf16), boths[0][at])
        for k in range(1, NX):
            total = total + dot(rows[k].astype(bf16), boths[k][at])
        out_ref[...] = ADAPTER_SCALE * total
    sq_a = ga_ref[...] * ga_ref[...] + SQ_EPS
    sq_b = gb_ref[...] * gb_ref[...] + SQ_EPS
    row_new = BETA_TWO * row_ref[...] + (1.0 - BETA_TWO) * (
        jnp.sum(sq_a.reshape(OWNED, RANK, WIDTH), axis=1) / RANK
    )
    row_out[...] = row_new
    col_out[...] = BETA_TWO * col_ref[...] + (1.0 - BETA_TWO) * (
        jnp.sum(sq_b.reshape(OWNED, RANK, WIDTH), axis=1) / RANK
    )
    lane = lax.broadcasted_iota(i32, (OWNED * RANK, 128), 1)
    columns = [jnp.sum(v, axis=1, keepdims=True) for v in (sq_a, sq_b, lift(row_new, WIDTH))]
    mixed = jnp.where(lane == 0, columns[0], jnp.where(lane == 1, columns[1], columns[2]))
    sum_ref[...] = mixed.T[:8]


def slots_kernel(slot, spots, smalls, boths, row, col):
    n = OWNED * RANK
    return pl.pallas_call(
        slots_body,
        in_specs=[SMEM] * 2 + [VMEM] * (2 * NX + 2),
        out_specs=[VMEM] * 5,
        out_shape=[like((n, WIDTH), f32)] * 2
        + [like((OWNED, WIDTH), f32)] * 2
        + [like((8, n), f32)],
        compiler_params=params(),
        cost_estimate=cost(2**27, 2**21),
    )(slot, spots, *smalls, *boths, row, col)


def update_body(p_ref, q_ref, ga_ref, gb_ref, row_ref, col_ref, dcol_ref, urow_ref, ua_ref, ub_ref, ca_ref, rb_ref):
    total = p_ref[...] + q_ref[...]
    col_a = BETA_TWO * dcol_ref[...] + (1.0 - BETA_TWO) * (total[0:1] / FULL)
    row_b = BETA_TWO * urow_ref[...] + (1.0 - BETA_TWO) * (total[1:2] / FULL)
    ca_ref[...] = col_a
    rb_ref[...] = row_b
    col_a = row_to_columns(col_a)[:, :1]
    row_b = row_to_columns(row_b)
    mean_a = row_to_columns(total[2:3])[:, :1] / FULL
    mean_b = lift(jnp.sum(row_b.reshape(OWNED, RANK, 128), axis=1), 128)[:, :1] / RANK
    ua_ref[...] = ga_ref[...] * lax.rsqrt(lift(row_ref[...], WIDTH) * col_a / mean_a)
    ub_ref[...] = gb_ref[...] * lax.rsqrt(row_b[:, :1] * lift(col_ref[...], WIDTH) / mean_b)


def update_kernel(p, q, ga, gb, row, col, dcol, urow):
    n = OWNED * RANK
    return pl.pallas_call(
        update_body,
        in_specs=[VMEM] * 8,
        out_specs=[VMEM] * 4,
        out_shape=[like((n, WIDTH), f32)] * 2 + [like((1, n), f32)] * 2,
        compiler_params=params(),
        cost_estimate=cost(2**20, 2**20),
    )(p, q, ga, gb, row, col, dcol, urow)


def add_body(a_ref, b_ref, *refs):
    refs[-1][...] = a_ref[...] + b_ref[...]


def add_kernel(a, b, *tokens):
    return pl.pallas_call(
        add_body,
        in_specs=[VMEM] * 2 + [HBM] * len(tokens),
        out_specs=VMEM,
        out_shape=like(a.shape, a.dtype),
        compiler_params=params(),
    )(a, b, *tokens)


def all_sum(v, core, *tokens):
    v = v + swap(v)
    a = lax.ppermute(v, F, plane_moves(lambda z, y, c: (z, y ^ (1 + c), c)))
    b = lax.ppermute(v, F, plane_moves(lambda z, y, c: (z, y ^ 3, c) if c else None))
    q = jnp.where(core == 0, v + a, a + b)
    v = add_kernel(q, swap(q), *tokens)
    a, b, d = [
        lax.ppermute(v, F, plane_moves(lambda z, y, c: (z ^ (k + 3 * c), y, c)))
        for k in (1, 2, 3)
    ]
    e = lax.ppermute(v, F, plane_moves(lambda z, y, c: (z ^ 7, y, c) if c else None))
    q = jnp.where(core == 0, (v + a) + (b + d), (a + b) + (d + e))
    return q, swap(q)


def on_device(
    inputs,
    norm_gain_vector,
    weight,
    down_adapters,
    up_adapters,
    tenant,
    tenant_slot_index,
    live_row_count,
    cotangent,
    down_row_factor,
    down_column_factor,
    up_row_factor,
    up_column_factor,
):
    dp = lax.axis_index("dp")
    z, y, core = lax.axis_index("z"), lax.axis_index("y"), lax.axis_index("core")
    opposite = 1 - core
    sign = 1 - 2 * core
    y_two, y_keep, y_send = (y + 2) % NY, (y + 1 + 2 * core) % NY, (y + 3 + 2 * core) % NY
    z_steps = [(z + NZ - s * sign * way) % NZ for s in (1, 2, 3) for way in (1, -1)]
    z_far = (z + NZ // 2) % NZ
    spots = jnp.stack(
        [y_two, opposite, y_send, core, y_send, opposite, y, opposite]
        + [y_two, core, y_keep, opposite, y_keep, core, y, core]
        + [z, y, core, dp]
        + z_steps
        + [z_far * 2 + core, z_far * 2 + opposite]
    ).astype(i32)
    down = down_adapters.transpose(1, 2, 0).reshape(TENANTS * RANK, WIDTH)
    up = up_adapters.reshape(TENANTS * RANK, WIDTH)
    tenant = tenant.reshape(1, ROWS)
    w5 = weight.reshape(NZ, NY, NC, WIDTH, WIDTH)
    w4 = weight.reshape(NZ, NY * NC, WIDTH, WIDTH)
    w_half = weight.reshape(NZ * 2, NY * NC // 2, WIDTH, WIDTH)

    gained, grad, turned = rows_kernel(
        live_row_count, inputs, norm_gain_vector.reshape(1, WIDTH), cotangent
    )
    own = [gained] + [lax.ppermute(gained, "y", turn(NY, k)) for k in (3, 2, 1)]
    other = [swap(v) for v in own]
    packed = inner_kernel(inputs, gained, grad, down, up, tenant)

    s_two, s_far, s_near, s_own = part_kernel(w5, turned, spots, 0, [[], [], [], []], [])
    r_two, r_far, r_near, r_own = [swap(v) for v in (s_two, s_far, s_near, s_own)]

    block, both = block_kernel(spots, own, other, grad)
    one = lax.ppermute(block, F, Z_BY_CORE)
    one_o = swap(one)
    two = lax.ppermute(one, F, Z_BY_CORE)
    two_o = swap(two)
    three = lax.ppermute(two, F, Z_BY_CORE)
    three_o = swap(three)
    half = jnp.where(core == 0, three[: NY * NC // 2], three[NY * NC // 2 :])
    four = lax.ppermute(half, F, Z_BY_CORE)
    four_o = swap(four)

    t_two, t_far = part_kernel(w5, turned, spots, 4, [[r_two], [r_far]], [block])
    g_two = lax.ppermute(t_two, F, Y_BY_CORE)
    g_far = lax.ppermute(t_far, F, Y_BY_CORE)
    (t_near,) = part_kernel(w5, turned, spots, 6, [[r_near, g_two]], [one])
    g_near = lax.ppermute(t_near, F, Y_BY_CORE)
    reduced = last_part_kernel(w5, turned, spots, 7, [r_own, swap(g_far), g_near], [two])
    pieces = [reduced[0]] + [
        lax.ppermute(reduced[k], "z", turn(NZ, k)) for k in (4, 3, 5, 2, 6, 1, 7)
    ]

    boths = [both] + [lax.ppermute(both, "dp", turn(NX, k)) for k in (1, 3, 2)]
    p, q = all_sum(packed, core, block)
    small, back, scale = small_kernel(p, q, tenant)
    smalls = [small] + [lax.ppermute(small, "dp", turn(NX, k)) for k in (1, 3, 2)]

    frozen = frozen_kernel(w4, spots, None, [block], [16])
    frozen = frozen_kernel(w4, spots, frozen, [one, one_o], [20, 21])
    frozen = frozen_kernel(w4, spots, frozen, [two, two_o], [22, 23])
    frozen = frozen_kernel(w4, spots, frozen, [three, three_o], [24, 25])
    projected = final_kernel(w_half, spots, frozen, four, four_o, scale, small, up, tenant)

    normed_gradient_transposed = gradient_kernel(pieces, down, back, tenant)

    ga, gb, row_a_new, col_b_new, moments = slots_kernel(
        tenant_slot_index, spots, smalls, boths, down_row_factor, up_column_factor
    )
    p, q = all_sum(moments, core)
    n = OWNED * RANK
    update_a, update_b, col_a_new, row_b_new = update_kernel(
        p,
        q,
        ga,
        gb,
        row_a_new,
        col_b_new,
        down_column_factor.reshape(1, n),
        up_row_factor.reshape(1, n),
    )
    return (
        projected,
        normed_gradient_transposed,
        update_a.reshape(OWNED, RANK, WIDTH).swapaxes(1, 2),
        update_b.reshape(OWNED, RANK, WIDTH),
        row_a_new,
        col_a_new.reshape(OWNED, RANK),
        row_b_new.reshape(OWNED, RANK),
        col_b_new,
    )


def solution(mesh):
    split = Mesh(mesh.devices.reshape(NX, NZ, NY, NC), ("dp",) + F)
    return jax.shard_map(
        on_device,
        mesh=split,
        in_specs=(
            P("dp", F),
            P(F),
            P(None, F),
            P(F, None, None),
            P(None, None, F),
            P("dp"),
            P(),
            P("dp"),
            P("dp", F),
            P("dp", F),
            P("dp", None),
            P("dp", None),
            P("dp", F),
        ),
        out_specs=(
            P("dp", F),
            P(F, "dp"),
            P("dp", F, None),
            P("dp", None, F),
            P("dp", F),
            P("dp", None),
            P("dp", None),
            P("dp", F),
        ),
        check_vma=False,
    )
```

```python
import functools

import jax
import jax.numpy as jnp
from jax import lax
from jax.experimental import pallas as pl
from jax.experimental.pallas import tpu as pltpu
from jax.sharding import Mesh, PartitionSpec as P

ADAPTER_SCALE = 0.5
BETA_TWO = 0.9
SQ_EPS = 1e-30
RMS_EPS = 1e-05
NX, NZ, NY, NC = 4, 8, 4, 2
F = ("z", "y", "core")
bf16, f32, i32 = jnp.bfloat16, jnp.float32, jnp.int32
NT = (((1,), (1,)), ((), ()))
NN = (((1,), (0,)), ((), ()))
TN = (((0,), (0,)), ((), ()))
ROWS, WIDTH, FULL, TENANTS, RANK, OWNED = 128, 256, 16384, 16, 32, 8
HBM = pl.BlockSpec(memory_space=pl.ANY)
VMEM = pl.BlockSpec(memory_space=pltpu.VMEM)
SMEM = pl.BlockSpec(memory_space=pltpu.SMEM)


def plane_moves(rule):
    pairs = []
    for z in range(NZ):
        for y in range(NY):
            for c in range(NC):
                to = rule(z, y, c)
                if to is not None:
                    z2, y2, c2 = to
                    pairs.append(
                        ((z * NY + y) * NC + c, ((z2 % NZ) * NY + y2 % NY) * NC + c2)
                    )
    return pairs


Z_BY_CORE = plane_moves(lambda z, y, c: (z + 1 - 2 * c, y, c))
Y_BY_CORE = plane_moves(lambda z, y, c: (z, y + 1 - 2 * c, c))


def turn(n, k):
    return [(i, (i + k) % n) for i in range(n)]


def swap(v):
    return lax.ppermute(v, "core", turn(NC, 1))


def like(shape, dtype):
    return jax.ShapeDtypeStruct(shape, dtype)


def tile_of(v):
    return pl.BlockSpec(v.shape, lambda *_, n=v.ndim: (0,) * n)


def whole(shape):
    return pl.BlockSpec(shape, lambda *_, n=len(shape): (0,) * n)


def params(n=48):
    return pltpu.CompilerParams(vmem_limit_bytes=n * 1024 * 1024)


def cost(flops, moved):
    return pl.CostEstimate(flops=flops, bytes_accessed=moved, transcendentals=0)


def dot(a, b, dims=NN):
    return lax.dot_general(a, b, dims, preferred_element_type=f32)


def column_to_rows(v):
    return jnp.broadcast_to(v, (v.shape[0], 128)).T


def row_to_columns(v):
    return jnp.broadcast_to(v, (128, v.shape[1])).T


def split_store(ref, at, v):
    n = v.shape[0]
    high = v.astype(bf16)
    ref[at : at + n] = high
    ref[at + n : at + 2 * n] = (v - high.astype(f32)).astype(bf16)


def split_load(ref, at, n):
    return ref[at : at + n].astype(f32) + ref[at + n : at + 2 * n].astype(f32)


PACKED = 2 * RANK + 16
MESSAGE = 2 * ROWS + 2 * PACKED


def rows_body(live_ref, x_ref, gain_ref, cot_ref, down_ref, up_ref, tenant_ref, message_ref, both_ref, turned_ref):
    x = x_ref[...].astype(f32)
    gained = (x * gain_ref[...].astype(f32)[None, :]).astype(bf16)
    at = lax.broadcasted_iota(i32, (ROWS, WIDTH), 0)
    grad = jnp.where(at < live_ref[0], cot_ref[...].astype(f32), 0.0)
    turned_ref[...] = grad.T.astype(bf16)
    grad = grad.astype(bf16)
    for k in range(NX):
        both_ref[k, 0] = gained
        both_ref[k, 1] = grad
    message_ref[:ROWS] = gained[:, :128]
    message_ref[ROWS : 2 * ROWS] = gained[:, 128:]
    tenant = tenant_ref[...]
    parts = []
    for w_ref, v in ((down_ref, gained), (up_ref, grad)):
        every = dot(w_ref[...], v, NT)
        picked = jnp.zeros((RANK, ROWS), f32)
        for t in range(TENANTS):
            picked = picked + jnp.where(tenant == t, every[t * RANK : (t + 1) * RANK], 0.0)
        parts.append(picked)
    parts.append(column_to_rows(jnp.sum(x * x, axis=1, keepdims=True))[:16])
    split_store(message_ref, 2 * ROWS, jnp.concatenate(parts))


def rows_kernel(live, x, gain, cot, down, up, tenant):
    return pl.pallas_call(
        rows_body,
        grid=(1,),
        in_specs=[SMEM] + [tile_of(v) for v in (x, gain, cot, down, up, tenant)],
        out_specs=[whole((MESSAGE, 128)), whole((NX, 2, ROWS, WIDTH)), whole((WIDTH, ROWS))],
        out_shape=[
            like((MESSAGE, 128), bf16),
            like((NX, 2, ROWS, WIDTH), bf16),
            like((WIDTH, ROWS), bf16),
        ],
        compiler_params=params(60),
        cost_estimate=cost(2**26, 2**20),
    )(live, x, gain, cot, down, up, tenant)


def part_body(counts, spots_ref, turned_ref, *refs):
    n = len(counts)
    refs = list(refs)
    w = [refs.pop(0) for _ in range(n)]
    adds = [[refs.pop(0) for _ in range(k)] for k in counts]
    outs = refs[len(refs) - n :]
    turned = turned_ref[...]
    for i in range(n):
        many = w[i].shape[0]
        total = dot(w[i][...].reshape(many * WIDTH, WIDTH), turned)
        for a in adds[i]:
            total = total + a[...].reshape(many * WIDTH, ROWS).astype(f32)
        outs[i][...] = total.astype(bf16).reshape(many, WIDTH, ROWS)


def part_kernel(w5, turned, spots, first, adds, tokens, tiles=2):
    n = len(adds)
    step = NZ // tiles
    w_specs = [
        pl.BlockSpec(
            (step, 1, 1, WIDTH, WIDTH),
            lambda i, s, k=k: (i, s[2 * (first + k)], s[2 * (first + k) + 1], 0, 0),
        )
        for k in range(n)
    ]
    tile = pl.BlockSpec((step, WIDTH, ROWS), lambda i, s: (i, 0, 0))
    flat = [a for some in adds for a in some]
    return pl.pallas_call(
        functools.partial(part_body, [len(a) for a in adds]),
        grid_spec=pltpu.PrefetchScalarGridSpec(
            num_scalar_prefetch=1,
            grid=(tiles,),
            in_specs=[pl.BlockSpec((WIDTH, ROWS), lambda i, s: (0, 0))]
            + w_specs
            + [tile] * len(flat)
            + [HBM] * len(tokens),
            out_specs=[tile] * n,
        ),
        out_shape=[like((NZ, WIDTH, ROWS), bf16)] * n,
        compiler_params=params(),
        cost_estimate=cost(n * 2**27, n * 2**21),
    )(spots, turned, *([w5] * n), *flat, *tokens)


MOMENTS = 2 * 8
PIECE = WIDTH + 2 * MOMENTS
ORDER = (0, 4, 3, 5, 2, 6, 1, 7)


def last_part_body(offsets, spots_ref, turned_ref, w_ref, a_ref, b_ref, c_ref, p_ref, q_ref, *refs):
    outs = refs[len(refs) - len(offsets) :]
    z = spots_ref[16]
    moments = p_ref[...] + q_ref[...]
    moments = jnp.concatenate([moments[:, :128], moments[:, 128:]])
    for k, out in zip(offsets, outs):
        at = (z + k) % NZ
        t = dot(w_ref[at, 0, 0], turned_ref[...])
        for a in (a_ref, b_ref, c_ref):
            t = t + a[at].astype(f32)
        out[:WIDTH] = t.astype(bf16)
        split_store(out, WIDTH, moments)


def last_part_kernel(w5, turned, spots, at, offsets, adds, moments, tokens):
    flat = pl.BlockSpec((WIDTH, ROWS), lambda i, s: (0, 0))
    wide = pl.BlockSpec((8, OWNED * RANK), lambda i, s: (0, 0))
    out = pl.BlockSpec((PIECE, ROWS), lambda i, s: (0, 0))
    return pl.pallas_call(
        functools.partial(last_part_body, offsets),
        grid_spec=pltpu.PrefetchScalarGridSpec(
            num_scalar_prefetch=1,
            grid=(1,),
            in_specs=[
                flat,
                pl.BlockSpec(
                    (NZ, 1, 1, WIDTH, WIDTH), lambda i, s: (0, s[2 * at], s[2 * at + 1], 0, 0)
                ),
            ]
            + [whole((NZ, WIDTH, ROWS))] * 3
            + [wide] * 2
            + [HBM] * len(tokens),
            out_specs=[out] * len(offsets),
        ),
        out_shape=[like((PIECE, ROWS), bf16)] * len(offsets),
        compiler_params=params(),
        cost_estimate=cost(2**27, 2**21),
    )(spots, turned, w5, *adds, *moments, *tokens)


BLOCK = NY * NC * 2 * ROWS
TAIL = 2 * ROWS


def block_body(spots_ref, *refs):
    own, other = refs[:NY], refs[NY : 2 * NY]
    block_ref, parts_ref = refs[-2:]
    y, core = spots_ref[17], spots_ref[18]
    for j in range(NY):
        at = ((y + j) % NY) * NC
        for spot, ref in ((at + core, own[j]), (at + 1 - core, other[j])):
            block_ref[pl.ds(pl.multiple_of(spot * 2 * ROWS, 2 * ROWS), 2 * ROWS)] = ref[
                : 2 * ROWS
            ]
            parts_ref[spot] = split_load(ref, 2 * ROWS, PACKED)
    total = parts_ref[0]
    for k in range(1, NY * NC):
        total = total + parts_ref[k]
    split_store(block_ref, BLOCK, total)
    block_ref[BLOCK + 2 * PACKED :] = jnp.zeros((TAIL - 2 * PACKED, 128), bf16)


def block_kernel(spots, own, other, *tokens):
    return pl.pallas_call(
        block_body,
        in_specs=[SMEM] + [VMEM] * (2 * NY) + [HBM] * len(tokens),
        out_specs=VMEM,
        out_shape=like((BLOCK + TAIL, 128), bf16),
        scratch_shapes=[pltpu.VMEM((NY * NC, PACKED, ROWS), f32)],
        compiler_params=params(),
    )(spots, *own, *other, *tokens)


def long_dot(x_ref, w_ref):
    many = x_ref.shape[0] // ROWS
    x = jnp.concatenate([x_ref[g * ROWS : (g + 1) * ROWS] for g in range(many)], axis=1)
    return dot(x, w_ref[...].reshape(many * 128, WIDTH))


def frozen_body(n, has_acc, spots_ref, *refs):
    refs = list(refs)
    acc_ref = refs.pop(0) if has_acc else None
    xs, ws, out_ref = refs[:n], refs[n : 2 * n], refs[-1]
    total = None
    for x_ref, w_ref in zip(xs, ws):
        term = long_dot(x_ref, w_ref)
        total = term if total is None else total + term

    @pl.when(pl.program_id(0) == 0)
    def _():
        out_ref[...] = total + acc_ref[...] if has_acc else total

    @pl.when(pl.program_id(0) > 0)
    def _():
        out_ref[...] = out_ref[...] + total


def frozen_kernel(w4, spots, acc, blocks, ats, tokens=(), tiles=2):
    n = len(blocks)
    flat = pl.BlockSpec((ROWS, WIDTH), lambda i, s: (0, 0))
    step = NY * NC // tiles
    has_acc = acc is not None
    return pl.pallas_call(
        functools.partial(frozen_body, n, has_acc),
        grid_spec=pltpu.PrefetchScalarGridSpec(
            num_scalar_prefetch=1,
            grid=(tiles,),
            in_specs=[flat] * has_acc
            + [pl.BlockSpec((step * 2 * ROWS, 128), lambda i, s: (i, 0))] * n
            + [
                pl.BlockSpec((1, step, WIDTH, WIDTH), lambda i, s, a=a: (s[a], i, 0, 0))
                for a in ats
            ]
            + [HBM] * len(tokens),
            out_specs=flat,
        ),
        out_shape=like((ROWS, WIDTH), f32),
        compiler_params=params(),
        cost_estimate=cost(n * 2**27, 9 * 2**20),
    )(spots, *([acc] * has_acc), *blocks, *([w4] * n), *tokens)


def final_body(spots_ref, acc_ref, x_ref, w_ref, scale_ref, small_ref, up_ref, tenant_ref, out_ref):
    total = acc_ref[...] + long_dot(x_ref, w_ref)
    tenant = tenant_ref[...]
    inner = small_ref[0, :RANK].astype(f32)
    spread = jnp.concatenate([jnp.where(tenant == t, inner, 0.0) for t in range(TENANTS)])
    adapted = dot(spread.T.astype(bf16), up_ref[...])
    scale = row_to_columns(scale_ref[:1])[:, :1]
    out_ref[...] = (scale * total + ADAPTER_SCALE * adapted).astype(bf16)


def final_kernel(w4, spots, acc, x, at, scale, small, up, tenant):
    def full(v):
        return pl.BlockSpec(v.shape, lambda i, s, n=v.ndim: (0,) * n)

    return pl.pallas_call(
        final_body,
        grid_spec=pltpu.PrefetchScalarGridSpec(
            num_scalar_prefetch=1,
            grid=(1,),
            in_specs=[
                full(acc),
                pl.BlockSpec((BLOCK, 128), lambda i, s: (0, 0)),
                pl.BlockSpec((1, NY * NC, WIDTH, WIDTH), lambda i, s: (s[at], 0, 0, 0)),
            ]
            + [full(v) for v in (scale, small, up, tenant)],
            out_specs=full(acc),
        ),
        out_shape=like((ROWS, WIDTH), bf16),
        compiler_params=params(),
        cost_estimate=cost(2**28, 9 * 2**20),
    )(spots, acc, x, w4, scale, small, up, tenant)


def gradient_body(*refs):
    pieces, (down_ref, back_ref, tenant_ref), out_ref = refs[:NZ], refs[NZ : NZ + 3], refs[-1]
    total = pieces[0][:WIDTH].astype(f32)
    for p in pieces[1:]:
        total = total + p[:WIDTH].astype(f32)
    tenant = tenant_ref[...]
    back = back_ref[...].astype(f32)
    spread = jnp.concatenate([jnp.where(tenant == t, back, 0.0) for t in range(TENANTS)])
    adapter = dot(down_ref[...].astype(f32).T.astype(bf16), spread.astype(bf16))
    out_ref[...] = (total + ADAPTER_SCALE * adapter).astype(bf16)


def gradient_kernel(pieces, down, back, tenant, *tokens):
    return pl.pallas_call(
        gradient_body,
        grid=(1,),
        in_specs=[VMEM] * NZ + [tile_of(v) for v in (down, back, tenant)] + [HBM] * len(tokens),
        out_specs=VMEM,
        out_shape=like((WIDTH, ROWS), bf16),
        compiler_params=params(),
        cost_estimate=cost(2**25, 2**20),
    )(*pieces, down, back, tenant, *tokens)


def small_body(spots_ref, *refs):
    parts, tenant_ref = refs[:NZ], refs[NZ]
    small_ref, back_ref, scale_ref, all_ref = refs[-4:]
    for at, ref in zip((16, 20, 21, 22, 23, 24, 25, 26), parts):
        all_ref[spots_ref[at]] = split_load(ref, 0, PACKED)
    total = all_ref[0]
    for k in range(1, NZ):
        total = total + all_ref[k]
    scale = lax.rsqrt(total[2 * RANK : 2 * RANK + 1] / FULL + RMS_EPS)
    back = total[RANK : 2 * RANK]
    for k in range(NX):
        small_ref[k, :RANK] = (total[:RANK] * scale).astype(bf16)
        small_ref[k, RANK : 2 * RANK] = (back * scale).astype(bf16)
        small_ref[k, 2 * RANK :] = jnp.broadcast_to(
            tenant_ref[...].astype(f32), (16, ROWS)
        ).astype(bf16)
    back_ref[...] = back.astype(bf16)
    scale_ref[...] = jnp.broadcast_to(scale, (8, ROWS))


def small_kernel(spots, blocks, tenant, *tokens):
    return pl.pallas_call(
        small_body,
        grid=(1,),
        in_specs=[SMEM]
        + [pl.BlockSpec((TAIL, 128), lambda i: (BLOCK // TAIL, 0))] * NZ
        + [tile_of(tenant)]
        + [HBM] * len(tokens),
        out_specs=[whole((NX, 2 * RANK + 16, ROWS)), whole((RANK, ROWS)), whole((8, ROWS))],
        out_shape=[
            like((NX, 2 * RANK + 16, ROWS), bf16),
            like((RANK, ROWS), bf16),
            like((8, ROWS), f32),
        ],
        scratch_shapes=[pltpu.VMEM((NZ, PACKED, ROWS), f32)],
        compiler_params=params(),
    )(spots, *blocks, tenant, *tokens)


def lift(v, size):
    return jnp.broadcast_to(v[:, None, :], (OWNED, RANK, size)).reshape(OWNED * RANK, size)


def slots_body(slot_ref, spots_ref, *refs):
    smalls, boths, row_ref, col_ref = refs[:4]
    ga_ref, gb_ref, row_out, col_out, sum_ref = refs[-5:]
    first = spots_ref[19] * OWNED
    a_rows, b_rows = [], []
    for k in range(NX):
        small_ref = smalls.at[k]
        tenant = small_ref[2 * RANK : 2 * RANK + 16].astype(f32)[:1]
        slot = jnp.full((1, ROWS), -1, i32)
        for t in range(TENANTS):
            slot = jnp.where(tenant == t, slot_ref[t], slot)
        inner = small_ref[:RANK].astype(f32)
        back = small_ref[RANK : 2 * RANK].astype(f32)
        a_rows.append(
            jnp.concatenate([jnp.where(slot == first + s, back, 0.0) for s in range(OWNED)])
        )
        b_rows.append(
            jnp.concatenate([jnp.where(slot == first + s, inner, 0.0) for s in range(OWNED)])
        )
    for rows, at, out_ref in ((a_rows, 0, ga_ref), (b_rows, 1, gb_ref)):
        total = dot(rows[0].astype(bf16), boths[0, at])
        for k in range(1, NX):
            total = total + dot(rows[k].astype(bf16), boths[k, at])
        out_ref[...] = ADAPTER_SCALE * total
    sq_a = ga_ref[...] * ga_ref[...] + SQ_EPS
    sq_b = gb_ref[...] * gb_ref[...] + SQ_EPS
    row_new = BETA_TWO * row_ref[...] + (1.0 - BETA_TWO) * (
        jnp.sum(sq_a.reshape(OWNED, RANK, WIDTH), axis=1) / RANK
    )
    row_out[...] = row_new
    col_out[...] = BETA_TWO * col_ref[...] + (1.0 - BETA_TWO) * (
        jnp.sum(sq_b.reshape(OWNED, RANK, WIDTH), axis=1) / RANK
    )
    lane = lax.broadcasted_iota(i32, (OWNED * RANK, 128), 1)
    columns = [jnp.sum(v, axis=1, keepdims=True) for v in (sq_a, sq_b, lift(row_new, WIDTH))]
    mixed = jnp.where(lane == 0, columns[0], jnp.where(lane == 1, columns[1], columns[2]))
    sum_ref[...] = mixed.T[:8]


def slots_kernel(slot, spots, smalls, boths, row, col, *tokens):
    n = OWNED * RANK
    return pl.pallas_call(
        slots_body,
        grid=(1,),
        in_specs=[SMEM] * 2
        + [tile_of(v) for v in (smalls, boths, row, col)]
        + [HBM] * len(tokens),
        out_specs=[whole((n, WIDTH))] * 2 + [whole((OWNED, WIDTH))] * 2 + [whole((8, n))],
        out_shape=[like((n, WIDTH), f32)] * 2
        + [like((OWNED, WIDTH), f32)] * 2
        + [like((8, n), f32)],
        compiler_params=params(60),
        cost_estimate=cost(2**27, 2**21),
    )(slot, spots, smalls, boths, row, col, *tokens)


def update_body(spots_ref, *refs):
    pieces = refs[:NZ]
    ga_ref, gb_ref, row_ref, col_ref, dcol_ref, urow_ref = refs[NZ : NZ + 6]
    ua_ref, ub_ref, ca_ref, rb_ref, parts_ref = refs[NZ + 6 :]
    z = spots_ref[16]
    for k, ref in zip(ORDER, pieces):
        parts_ref[(z + NZ - k) % NZ] = split_load(ref, WIDTH, MOMENTS)
    total = parts_ref[0]
    for k in range(1, NZ):
        total = total + parts_ref[k]
    total = jnp.concatenate([total[:8], total[8:]], axis=1)
    total = jnp.concatenate([total, jnp.zeros((120, 2 * ROWS), f32)]).T
    same = lax.broadcasted_iota(i32, (OWNED, RANK, RANK), 1) == lax.broadcasted_iota(
        i32, (OWNED, RANK, RANK), 2
    )

    def mixed(old_ref, sums, out_ref):
        old = jnp.where(same, old_ref[...][:, None, :], 0.0)
        old = jnp.sum(old, axis=2, keepdims=True).reshape(OWNED * RANK, 1)
        new = BETA_TWO * old + (1.0 - BETA_TWO) * (sums / FULL)
        back = jnp.broadcast_to(new, (OWNED * RANK, RANK)).reshape(OWNED, RANK, RANK)
        out_ref[...] = jnp.sum(jnp.where(same, back, 0.0), axis=1)
        return new

    col_a = mixed(dcol_ref, total[:, 0:1], ca_ref)
    row_b = mixed(urow_ref, total[:, 1:2], rb_ref)
    mean_a = total[:, 2:3] / FULL
    wide = jnp.broadcast_to(row_b, (OWNED * RANK, 128)).reshape(OWNED, RANK, 128)
    mean_b = lift(jnp.sum(wide, axis=1), 128)[:, :1] / RANK
    ua_ref[...] = ga_ref[...] * lax.rsqrt(lift(row_ref[...], WIDTH) * col_a / mean_a)
    ub_ref[...] = gb_ref[...] * lax.rsqrt(row_b * lift(col_ref[...], WIDTH) / mean_b)


def update_kernel(spots, pieces, ga, gb, row, col, dcol, urow):
    n = OWNED * RANK
    return pl.pallas_call(
        update_body,
        grid=(1,),
        in_specs=[SMEM] + [VMEM] * NZ + [tile_of(v) for v in (ga, gb, row, col, dcol, urow)],
        out_specs=[VMEM] * 4,
        out_shape=[like((n, WIDTH), f32)] * 2 + [like((OWNED, RANK), f32)] * 2,
        scratch_shapes=[pltpu.VMEM((NZ, MOMENTS, 128), f32)],
        compiler_params=params(),
        cost_estimate=cost(2**20, 2**20),
    )(spots, *pieces, ga, gb, row, col, dcol, urow)


def tied_body(*refs):
    pass


def tied(v, *tokens):
    return pl.pallas_call(
        tied_body,
        in_specs=[HBM] * (1 + len(tokens)),
        out_specs=HBM,
        out_shape=like(v.shape, v.dtype),
        input_output_aliases={0: 0},
        compiler_params=params(),
    )(v, *tokens)


def sum_y(v, core):
    v = v + swap(v)
    a = lax.ppermute(v, F, plane_moves(lambda z, y, c: (z, y ^ (1 + c), c)))
    b = lax.ppermute(v, F, plane_moves(lambda z, y, c: (z, y ^ 3, c) if c else None))
    q = jnp.where(core == 0, v + a, a + b)
    return q, swap(q)


def on_device(
    inputs,
    norm_gain_vector,
    weight,
    down_adapters,
    up_adapters,
    tenant,
    tenant_slot_index,
    live_row_count,
    cotangent,
    down_row_factor,
    down_column_factor,
    up_row_factor,
    up_column_factor,
):
    dp = lax.axis_index("dp")
    z, y, core = lax.axis_index("z"), lax.axis_index("y"), lax.axis_index("core")
    opposite = 1 - core
    sign = 1 - 2 * core
    y_two, y_keep, y_send = (y + 2) % NY, (y + 1 + 2 * core) % NY, (y + 3 + 2 * core) % NY
    z_steps = [(z + NZ - s * sign * way) % NZ for s in (1, 2, 3) for way in (1, -1)]
    z_far = (z + NZ // 2) % NZ
    spots = jnp.stack(
        [y_two, opposite, y_send, core, y_send, opposite, y, opposite]
        + [y_two, core, y_keep, opposite, y_keep, core, y, core]
        + [z, y, core, dp]
        + z_steps
        + [z_far]
    ).astype(i32)
    down = down_adapters.transpose(1, 2, 0).reshape(TENANTS * RANK, WIDTH)
    up = up_adapters.reshape(TENANTS * RANK, WIDTH)
    tenant = tenant.reshape(1, ROWS)
    w5 = weight.reshape(NZ, NY, NC, WIDTH, WIDTH)
    w4 = weight.reshape(NZ, NY * NC, WIDTH, WIDTH)

    message, both, turned = rows_kernel(
        live_row_count, inputs, norm_gain_vector, cotangent, down, up, tenant
    )
    s_two, s_far = part_kernel(w5, turned, spots, 0, [[], []], [])
    own = [message] + [lax.ppermute(message, "y", turn(NY, k)) for k in (3, 2, 1)]
    own[1] = tied(own[1], s_two)
    other = [swap(v) for v in own]
    boths = lax.all_to_all(both, "dp", 0, 0, tiled=True)

    block = block_kernel(spots, own, other)
    s_near, s_own = part_kernel(w5, turned, spots, 2, [[], []], [block])
    r_two, r_far, r_near, r_own = [swap(v) for v in (s_two, s_far, s_near, s_own)]
    t_two, t_far = part_kernel(w5, turned, spots, 4, [[r_two], [r_far]], [block])
    g_two = lax.ppermute(t_two, F, Y_BY_CORE)
    g_far = lax.ppermute(t_far, F, Y_BY_CORE)
    frozen_zero = frozen_kernel(w4, spots, None, [block], [16])

    one = tied(lax.ppermute(block, F, Z_BY_CORE), t_far, s_near)
    one_o = swap(one)
    two = lax.ppermute(one, F, Z_BY_CORE)
    (t_near,) = part_kernel(w5, turned, spots, 6, [[r_near, g_two]], [])
    g_near = lax.ppermute(t_near, F, Y_BY_CORE)
    two = tied(two, t_near, frozen_zero, boths)
    two_o = swap(two)
    frozen_one = frozen_kernel(w4, spots, frozen_zero, [one, one_o], [20, 21])
    three = lax.ppermute(two, F, Z_BY_CORE)
    three = tied(three, frozen_one)
    three_o = swap(three)
    frozen_two = frozen_kernel(w4, spots, frozen_one, [two, two_o], [22, 23])
    four = lax.ppermute(three, F, Z_BY_CORE)
    four = tied(four, frozen_two)
    frozen_three = frozen_kernel(w4, spots, frozen_two, [three, three_o], [24, 25])

    small, back, scale = small_kernel(
        spots, [block, one, one_o, two, two_o, three, three_o, four], tenant
    )
    smalls = lax.all_to_all(small, "dp", 0, 0, tiled=True)
    projected = final_kernel(w4, spots, frozen_three, four, 26, scale, small, up, tenant)
    ga, gb, row_a_new, col_b_new, moments = slots_kernel(
        tenant_slot_index,
        spots,
        smalls,
        boths,
        down_row_factor,
        up_column_factor,
        projected,
    )
    moments = sum_y(moments, core)

    adds = [r_own, swap(g_far), g_near]
    first = last_part_kernel(w5, turned, spots, 7, ORDER[1:4], adds, moments, [])
    second = last_part_kernel(
        w5, turned, spots, 7, ORDER[4:] + ORDER[:1], adds, moments, [first[0]]
    )
    pieces = [second[-1]]
    for k, piece in zip(ORDER[1:], first + second[:-1]):
        pieces.append(lax.ppermute(piece, "z", turn(NZ, k)))
    normed_gradient_transposed = gradient_kernel(pieces, down, back, tenant)
    update_a, update_b, col_a_new, row_b_new = update_kernel(
        spots,
        pieces,
        ga,
        gb,
        row_a_new,
        col_b_new,
        down_column_factor,
        up_row_factor,
    )
    return (
        projected,
        normed_gradient_transposed,
        update_a.reshape(OWNED, RANK, WIDTH).swapaxes(1, 2),
        update_b.reshape(OWNED, RANK, WIDTH),
        row_a_new,
        col_a_new,
        row_b_new,
        col_b_new,
    )


def solution(mesh):
    split = Mesh(mesh.devices.reshape(NX, NZ, NY, NC), ("dp",) + F)
    return jax.shard_map(
        on_device,
        mesh=split,
        in_specs=(
            P("dp", F),
            P(F),
            P(None, F),
            P(F, None, None),
            P(None, None, F),
            P("dp"),
            P(),
            P("dp"),
            P("dp", F),
            P("dp", F),
            P("dp", None),
            P("dp", None),
            P("dp", F),
        ),
        out_specs=(
            P("dp", F),
            P(F, "dp"),
            P("dp", F, None),
            P("dp", None, F),
            P("dp", F),
            P("dp", None),
            P("dp", None),
            P("dp", F),
        ),
        check_vma=False,
    )
```

```python
import functools

import jax
import jax.numpy as jnp
from jax import lax
from jax.experimental import pallas as pl
from jax.experimental.pallas import tpu as pltpu
from jax.sharding import Mesh, PartitionSpec as P

ADAPTER_SCALE = 0.5
BETA_TWO = 0.9
SQ_EPS = 1e-30
RMS_EPS = 1e-05
NX, NZ, NY, NC = 4, 8, 4, 2
F = ("z", "y", "core")
bf16, f32, i32 = jnp.bfloat16, jnp.float32, jnp.int32
NT = (((1,), (1,)), ((), ()))
NN = (((1,), (0,)), ((), ()))
TN = (((0,), (0,)), ((), ()))
ROWS, WIDTH, FULL, TENANTS, RANK, OWNED = 128, 256, 16384, 16, 32, 8
HBM = pl.BlockSpec(memory_space=pl.ANY)
VMEM = pl.BlockSpec(memory_space=pltpu.VMEM)
SMEM = pl.BlockSpec(memory_space=pltpu.SMEM)


def plane_moves(rule):
    pairs = []
    for z in range(NZ):
        for y in range(NY):
            for c in range(NC):
                to = rule(z, y, c)
                if to is not None:
                    z2, y2, c2 = to
                    pairs.append(
                        ((z * NY + y) * NC + c, ((z2 % NZ) * NY + y2 % NY) * NC + c2)
                    )
    return pairs


Z_BY_CORE = plane_moves(lambda z, y, c: (z + 1 - 2 * c, y, c))
Y_BY_CORE = plane_moves(lambda z, y, c: (z, y + 1 - 2 * c, c))


def turn(n, k):
    return [(i, (i + k) % n) for i in range(n)]


def swap(v):
    return lax.ppermute(v, "core", turn(NC, 1))


def like(shape, dtype):
    return jax.ShapeDtypeStruct(shape, dtype)


def tile_of(v):
    return pl.BlockSpec(v.shape, lambda *_, n=v.ndim: (0,) * n)


def whole(shape):
    return pl.BlockSpec(shape, lambda *_, n=len(shape): (0,) * n)


def params(n=48):
    return pltpu.CompilerParams(vmem_limit_bytes=n * 1024 * 1024)


def cost(flops, moved):
    return pl.CostEstimate(flops=flops, bytes_accessed=moved, transcendentals=0)


def dot(a, b, dims=NN):
    return lax.dot_general(a, b, dims, preferred_element_type=f32)


def column_to_rows(v):
    return jnp.broadcast_to(v, (v.shape[0], 128)).T


def row_to_columns(v):
    return jnp.broadcast_to(v, (128, v.shape[1])).T


def split_store(ref, at, v):
    n = v.shape[0]
    high = v.astype(bf16)
    ref[at : at + n] = high
    ref[at + n : at + 2 * n] = (v - high.astype(f32)).astype(bf16)


def split_load(ref, at, n):
    return ref[at : at + n].astype(f32) + ref[at + n : at + 2 * n].astype(f32)


PACKED = 2 * RANK + 16
MESSAGE = 2 * ROWS + 2 * PACKED


def rows_body(live_ref, x_ref, gain_ref, cot_ref, down_ref, up_ref, tenant_ref, message_ref, both_ref, turned_ref):
    x = x_ref[...].astype(f32)
    gained = (x * gain_ref[...].astype(f32)[None, :]).astype(bf16)
    at = lax.broadcasted_iota(i32, (ROWS, WIDTH), 0)
    grad = jnp.where(at < live_ref[0], cot_ref[...].astype(f32), 0.0)
    turned_ref[...] = grad.T.astype(bf16)
    grad = grad.astype(bf16)
    for k in range(NX):
        both_ref[k, 0] = gained
        both_ref[k, 1] = grad
    message_ref[:ROWS] = gained[:, :128]
    message_ref[ROWS : 2 * ROWS] = gained[:, 128:]
    tenant = tenant_ref[...]
    parts = []
    for w_ref, v in ((down_ref, gained), (up_ref, grad)):
        every = dot(w_ref[...], v, NT)
        picked = jnp.zeros((RANK, ROWS), f32)
        for t in range(TENANTS):
            picked = picked + jnp.where(tenant == t, every[t * RANK : (t + 1) * RANK], 0.0)
        parts.append(picked)
    parts.append(column_to_rows(jnp.sum(x * x, axis=1, keepdims=True))[:16])
    split_store(message_ref, 2 * ROWS, jnp.concatenate(parts))


def rows_kernel(live, x, gain, cot, down, up, tenant):
    return pl.pallas_call(
        rows_body,
        grid=(1,),
        in_specs=[SMEM] + [tile_of(v) for v in (x, gain, cot, down, up, tenant)],
        out_specs=[whole((MESSAGE, 128)), whole((NX, 2, ROWS, WIDTH)), whole((WIDTH, ROWS))],
        out_shape=[
            like((MESSAGE, 128), bf16),
            like((NX, 2, ROWS, WIDTH), bf16),
            like((WIDTH, ROWS), bf16),
        ],
        compiler_params=params(60),
        cost_estimate=cost(2**26, 2**20),
    )(live, x, gain, cot, down, up, tenant)


def part_body(counts, spots_ref, turned_ref, *refs):
    n = len(counts)
    refs = list(refs)
    w = [refs.pop(0) for _ in range(n)]
    adds = [[refs.pop(0) for _ in range(k)] for k in counts]
    outs = refs[len(refs) - n :]
    turned = turned_ref[...]
    for i in range(n):
        many = w[i].shape[0]
        total = dot(w[i][...].reshape(many * WIDTH, WIDTH), turned)
        for a in adds[i]:
            total = total + a[...].reshape(many * WIDTH, ROWS).astype(f32)
        outs[i][...] = total.astype(bf16).reshape(many, WIDTH, ROWS)


def part_kernel(w5, turned, spots, first, adds, tokens, tiles=2):
    n = len(adds)
    step = NZ // tiles
    w_specs = [
        pl.BlockSpec(
            (step, 1, 1, WIDTH, WIDTH),
            lambda i, s, k=k: (i, s[2 * (first + k)], s[2 * (first + k) + 1], 0, 0),
        )
        for k in range(n)
    ]
    tile = pl.BlockSpec((step, WIDTH, ROWS), lambda i, s: (i, 0, 0))
    flat = [a for some in adds for a in some]
    return pl.pallas_call(
        functools.partial(part_body, [len(a) for a in adds]),
        grid_spec=pltpu.PrefetchScalarGridSpec(
            num_scalar_prefetch=1,
            grid=(tiles,),
            in_specs=[pl.BlockSpec((WIDTH, ROWS), lambda i, s: (0, 0))]
            + w_specs
            + [tile] * len(flat)
            + [HBM] * len(tokens),
            out_specs=[tile] * n,
        ),
        out_shape=[like((NZ, WIDTH, ROWS), bf16)] * n,
        compiler_params=params(),
        cost_estimate=cost(n * 2**27, n * 2**21),
    )(spots, turned, *([w5] * n), *flat, *tokens)


MOMENTS = 2 * 8
PIECE = WIDTH + 2 * MOMENTS
ORDER = (0, 4, 3, 5, 2, 6, 1, 7)


def last_part_body(offsets, spots_ref, turned_ref, w_ref, a_ref, b_ref, c_ref, p_ref, q_ref, *refs):
    outs = refs[len(refs) - len(offsets) :]
    z = spots_ref[16]
    moments = p_ref[...] + q_ref[...]
    moments = jnp.concatenate([moments[:, :128], moments[:, 128:]])
    for k, out in zip(offsets, outs):
        at = (z + k) % NZ
        t = dot(w_ref[at, 0, 0], turned_ref[...])
        for a in (a_ref, b_ref, c_ref):
            t = t + a[at].astype(f32)
        out[:WIDTH] = t.astype(bf16)
        split_store(out, WIDTH, moments)


def last_part_kernel(w5, turned, spots, at, offsets, adds, moments, tokens):
    flat = pl.BlockSpec((WIDTH, ROWS), lambda i, s: (0, 0))
    wide = pl.BlockSpec((8, OWNED * RANK), lambda i, s: (0, 0))
    out = pl.BlockSpec((PIECE, ROWS), lambda i, s: (0, 0))
    return pl.pallas_call(
        functools.partial(last_part_body, offsets),
        grid_spec=pltpu.PrefetchScalarGridSpec(
            num_scalar_prefetch=1,
            grid=(1,),
            in_specs=[
                flat,
                pl.BlockSpec(
                    (NZ, 1, 1, WIDTH, WIDTH), lambda i, s: (0, s[2 * at], s[2 * at + 1], 0, 0)
                ),
            ]
            + [whole((NZ, WIDTH, ROWS))] * 3
            + [wide] * 2
            + [HBM] * len(tokens),
            out_specs=[out] * len(offsets),
        ),
        out_shape=[like((PIECE, ROWS), bf16)] * len(offsets),
        compiler_params=params(),
        cost_estimate=cost(2**27, 2**21),
    )(spots, turned, w5, *adds, *moments, *tokens)


BLOCK = NY * NC * 2 * ROWS
TAIL = 2 * ROWS


def block_body(spots_ref, *refs):
    own, other = refs[:NY], refs[NY : 2 * NY]
    block_ref, parts_ref = refs[-2:]
    y, core = spots_ref[17], spots_ref[18]
    for j in range(NY):
        at = ((y + j) % NY) * NC
        for spot, ref in ((at + core, own[j]), (at + 1 - core, other[j])):
            block_ref[pl.ds(pl.multiple_of(spot * 2 * ROWS, 2 * ROWS), 2 * ROWS)] = ref[
                : 2 * ROWS
            ]
            parts_ref[spot] = split_load(ref, 2 * ROWS, PACKED)
    total = parts_ref[0]
    for k in range(1, NY * NC):
        total = total + parts_ref[k]
    split_store(block_ref, BLOCK, total)
    block_ref[BLOCK + 2 * PACKED :] = jnp.zeros((TAIL - 2 * PACKED, 128), bf16)


def block_kernel(spots, own, other, *tokens):
    return pl.pallas_call(
        block_body,
        in_specs=[SMEM] + [VMEM] * (2 * NY) + [HBM] * len(tokens),
        out_specs=VMEM,
        out_shape=like((BLOCK + TAIL, 128), bf16),
        scratch_shapes=[pltpu.VMEM((NY * NC, PACKED, ROWS), f32)],
        compiler_params=params(),
    )(spots, *own, *other, *tokens)


def long_dot(x_ref, w_ref):
    many = x_ref.shape[0] // ROWS
    x = jnp.concatenate([x_ref[g * ROWS : (g + 1) * ROWS] for g in range(many)], axis=1)
    return dot(x, w_ref[...].reshape(many * 128, WIDTH))


def frozen_body(n, has_acc, spots_ref, *refs):
    refs = list(refs)
    acc_ref = refs.pop(0) if has_acc else None
    xs, ws, out_ref = refs[:n], refs[n : 2 * n], refs[-1]
    total = None
    for x_ref, w_ref in zip(xs, ws):
        term = long_dot(x_ref, w_ref)
        total = term if total is None else total + term

    @pl.when(pl.program_id(0) == 0)
    def _():
        out_ref[...] = total + acc_ref[...] if has_acc else total

    @pl.when(pl.program_id(0) > 0)
    def _():
        out_ref[...] = out_ref[...] + total


def frozen_kernel(w4, spots, acc, blocks, ats, tokens=(), tiles=2):
    n = len(blocks)
    flat = pl.BlockSpec((ROWS, WIDTH), lambda i, s: (0, 0))
    step = NY * NC // tiles
    has_acc = acc is not None
    return pl.pallas_call(
        functools.partial(frozen_body, n, has_acc),
        grid_spec=pltpu.PrefetchScalarGridSpec(
            num_scalar_prefetch=1,
            grid=(tiles,),
            in_specs=[flat] * has_acc
            + [pl.BlockSpec((step * 2 * ROWS, 128), lambda i, s: (i, 0))] * n
            + [
                pl.BlockSpec((1, step, WIDTH, WIDTH), lambda i, s, a=a: (s[a], i, 0, 0))
                for a in ats
            ]
            + [HBM] * len(tokens),
            out_specs=flat,
        ),
        out_shape=like((ROWS, WIDTH), f32),
        compiler_params=params(),
        cost_estimate=cost(n * 2**27, 9 * 2**20),
    )(spots, *([acc] * has_acc), *blocks, *([w4] * n), *tokens)


def final_body(spots_ref, acc_ref, x_ref, w_ref, scale_ref, small_ref, up_ref, tenant_ref, out_ref):
    total = acc_ref[...] + long_dot(x_ref, w_ref)
    tenant = tenant_ref[...]
    inner = small_ref[0, :RANK].astype(f32)
    spread = jnp.concatenate([jnp.where(tenant == t, inner, 0.0) for t in range(TENANTS)])
    adapted = dot(spread.T.astype(bf16), up_ref[...])
    scale = row_to_columns(scale_ref[:1])[:, :1]
    out_ref[...] = (scale * total + ADAPTER_SCALE * adapted).astype(bf16)


def final_kernel(w4, spots, acc, x, at, scale, small, up, tenant):
    def full(v):
        return pl.BlockSpec(v.shape, lambda i, s, n=v.ndim: (0,) * n)

    return pl.pallas_call(
        final_body,
        grid_spec=pltpu.PrefetchScalarGridSpec(
            num_scalar_prefetch=1,
            grid=(1,),
            in_specs=[
                full(acc),
                pl.BlockSpec((BLOCK, 128), lambda i, s: (0, 0)),
                pl.BlockSpec((1, NY * NC, WIDTH, WIDTH), lambda i, s: (s[at], 0, 0, 0)),
            ]
            + [full(v) for v in (scale, small, up, tenant)],
            out_specs=full(acc),
        ),
        out_shape=like((ROWS, WIDTH), bf16),
        compiler_params=params(),
        cost_estimate=cost(2**28, 9 * 2**20),
    )(spots, acc, x, w4, scale, small, up, tenant)


def gradient_body(*refs):
    pieces, (down_ref, back_ref, tenant_ref), out_ref = refs[:NZ], refs[NZ : NZ + 3], refs[-1]
    total = pieces[0][:WIDTH].astype(f32)
    for p in pieces[1:]:
        total = total + p[:WIDTH].astype(f32)
    tenant = tenant_ref[...]
    back = back_ref[...].astype(f32)
    spread = jnp.concatenate([jnp.where(tenant == t, back, 0.0) for t in range(TENANTS)])
    adapter = dot(down_ref[...].astype(f32).T.astype(bf16), spread.astype(bf16))
    out_ref[...] = (total + ADAPTER_SCALE * adapter).astype(bf16)


def gradient_kernel(pieces, down, back, tenant, *tokens):
    return pl.pallas_call(
        gradient_body,
        grid=(1,),
        in_specs=[VMEM] * NZ + [tile_of(v) for v in (down, back, tenant)] + [HBM] * len(tokens),
        out_specs=VMEM,
        out_shape=like((WIDTH, ROWS), bf16),
        compiler_params=params(),
        cost_estimate=cost(2**25, 2**20),
    )(*pieces, down, back, tenant, *tokens)


def small_body(spots_ref, *refs):
    parts, tenant_ref = refs[:NZ], refs[NZ]
    small_ref, back_ref, scale_ref, all_ref = refs[-4:]
    for at, ref in zip((16, 20, 21, 22, 23, 24, 25, 26), parts):
        all_ref[spots_ref[at]] = split_load(ref, 0, PACKED)
    total = all_ref[0]
    for k in range(1, NZ):
        total = total + all_ref[k]
    scale = lax.rsqrt(total[2 * RANK : 2 * RANK + 1] / FULL + RMS_EPS)
    back = total[RANK : 2 * RANK]
    for k in range(NX):
        small_ref[k, :RANK] = (total[:RANK] * scale).astype(bf16)
        small_ref[k, RANK : 2 * RANK] = (back * scale).astype(bf16)
        small_ref[k, 2 * RANK :] = jnp.broadcast_to(
            tenant_ref[...].astype(f32), (16, ROWS)
        ).astype(bf16)
    back_ref[...] = back.astype(bf16)
    scale_ref[...] = jnp.broadcast_to(scale, (8, ROWS))


def small_kernel(spots, blocks, tenant, *tokens):
    return pl.pallas_call(
        small_body,
        grid=(1,),
        in_specs=[SMEM]
        + [pl.BlockSpec((TAIL, 128), lambda i: (BLOCK // TAIL, 0))] * NZ
        + [tile_of(tenant)]
        + [HBM] * len(tokens),
        out_specs=[whole((NX, 2 * RANK + 16, ROWS)), whole((RANK, ROWS)), whole((8, ROWS))],
        out_shape=[
            like((NX, 2 * RANK + 16, ROWS), bf16),
            like((RANK, ROWS), bf16),
            like((8, ROWS), f32),
        ],
        scratch_shapes=[pltpu.VMEM((NZ, PACKED, ROWS), f32)],
        compiler_params=params(),
    )(spots, *blocks, tenant, *tokens)


def lift(v, size):
    return jnp.broadcast_to(v[:, None, :], (OWNED, RANK, size)).reshape(OWNED * RANK, size)


def slots_body(slot_ref, spots_ref, *refs):
    smalls, boths, row_ref, col_ref = refs[:4]
    ga_ref, gb_ref, row_out, col_out, sum_ref = refs[-5:]
    first = spots_ref[19] * OWNED
    a_rows, b_rows = [], []
    for k in range(NX):
        small_ref = smalls.at[k]
        tenant = small_ref[2 * RANK : 2 * RANK + 16].astype(f32)[:1]
        slot = jnp.full((1, ROWS), -1, i32)
        for t in range(TENANTS):
            slot = jnp.where(tenant == t, slot_ref[t], slot)
        inner = small_ref[:RANK].astype(f32)
        back = small_ref[RANK : 2 * RANK].astype(f32)
        a_rows.append(
            jnp.concatenate([jnp.where(slot == first + s, back, 0.0) for s in range(OWNED)])
        )
        b_rows.append(
            jnp.concatenate([jnp.where(slot == first + s, inner, 0.0) for s in range(OWNED)])
        )
    for rows, at, out_ref in ((a_rows, 0, ga_ref), (b_rows, 1, gb_ref)):
        total = dot(rows[0].astype(bf16), boths[0, at])
        for k in range(1, NX):
            total = total + dot(rows[k].astype(bf16), boths[k, at])
        out_ref[...] = ADAPTER_SCALE * total
    sq_a = ga_ref[...] * ga_ref[...] + SQ_EPS
    sq_b = gb_ref[...] * gb_ref[...] + SQ_EPS
    row_new = BETA_TWO * row_ref[...] + (1.0 - BETA_TWO) * (
        jnp.sum(sq_a.reshape(OWNED, RANK, WIDTH), axis=1) / RANK
    )
    row_out[...] = row_new
    col_out[...] = BETA_TWO * col_ref[...] + (1.0 - BETA_TWO) * (
        jnp.sum(sq_b.reshape(OWNED, RANK, WIDTH), axis=1) / RANK
    )
    lane = lax.broadcasted_iota(i32, (OWNED * RANK, 128), 1)
    columns = [jnp.sum(v, axis=1, keepdims=True) for v in (sq_a, sq_b, lift(row_new, WIDTH))]
    mixed = jnp.where(lane == 0, columns[0], jnp.where(lane == 1, columns[1], columns[2]))
    sum_ref[...] = mixed.T[:8]


def slots_kernel(slot, spots, smalls, boths, row, col, *tokens):
    n = OWNED * RANK
    return pl.pallas_call(
        slots_body,
        grid=(1,),
        in_specs=[SMEM] * 2
        + [tile_of(v) for v in (smalls, boths, row, col)]
        + [HBM] * len(tokens),
        out_specs=[whole((n, WIDTH))] * 2 + [whole((OWNED, WIDTH))] * 2 + [whole((8, n))],
        out_shape=[like((n, WIDTH), f32)] * 2
        + [like((OWNED, WIDTH), f32)] * 2
        + [like((8, n), f32)],
        compiler_params=params(60),
        cost_estimate=cost(2**27, 2**21),
    )(slot, spots, smalls, boths, row, col, *tokens)


def update_body(spots_ref, *refs):
    pieces = refs[:NZ]
    ga_ref, gb_ref, row_ref, col_ref, dcol_ref, urow_ref = refs[NZ : NZ + 6]
    ua_ref, ub_ref, ca_ref, rb_ref, parts_ref = refs[NZ + 6 :]
    z = spots_ref[16]
    for k, ref in zip(ORDER, pieces):
        parts_ref[(z + NZ - k) % NZ] = split_load(ref, WIDTH, MOMENTS)
    total = parts_ref[0]
    for k in range(1, NZ):
        total = total + parts_ref[k]
    total = jnp.concatenate([total[:8], total[8:]], axis=1)
    total = jnp.concatenate([total, jnp.zeros((120, 2 * ROWS), f32)]).T
    same = lax.broadcasted_iota(i32, (OWNED, RANK, RANK), 1) == lax.broadcasted_iota(
        i32, (OWNED, RANK, RANK), 2
    )

    def mixed(old_ref, sums, out_ref):
        old = jnp.where(same, old_ref[...][:, None, :], 0.0)
        old = jnp.sum(old, axis=2, keepdims=True).reshape(OWNED * RANK, 1)
        new = BETA_TWO * old + (1.0 - BETA_TWO) * (sums / FULL)
        back = jnp.broadcast_to(new, (OWNED * RANK, RANK)).reshape(OWNED, RANK, RANK)
        out_ref[...] = jnp.sum(jnp.where(same, back, 0.0), axis=1)
        return new

    col_a = mixed(dcol_ref, total[:, 0:1], ca_ref)
    row_b = mixed(urow_ref, total[:, 1:2], rb_ref)
    mean_a = total[:, 2:3] / FULL
    wide = jnp.broadcast_to(row_b, (OWNED * RANK, 128)).reshape(OWNED, RANK, 128)
    mean_b = lift(jnp.sum(wide, axis=1), 128)[:, :1] / RANK
    ua_ref[...] = ga_ref[...] * lax.rsqrt(lift(row_ref[...], WIDTH) * col_a / mean_a)
    ub_ref[...] = gb_ref[...] * lax.rsqrt(row_b * lift(col_ref[...], WIDTH) / mean_b)


def update_kernel(spots, pieces, ga, gb, row, col, dcol, urow):
    n = OWNED * RANK
    return pl.pallas_call(
        update_body,
        grid=(1,),
        in_specs=[SMEM] + [VMEM] * NZ + [tile_of(v) for v in (ga, gb, row, col, dcol, urow)],
        out_specs=[VMEM] * 4,
        out_shape=[like((n, WIDTH), f32)] * 2 + [like((OWNED, RANK), f32)] * 2,
        scratch_shapes=[pltpu.VMEM((NZ, MOMENTS, 128), f32)],
        compiler_params=params(),
        cost_estimate=cost(2**20, 2**20),
    )(spots, *pieces, ga, gb, row, col, dcol, urow)


def tied_body(*refs):
    pass


def tied(v, *tokens):
    return pl.pallas_call(
        tied_body,
        in_specs=[HBM] * (1 + len(tokens)),
        out_specs=HBM,
        out_shape=like(v.shape, v.dtype),
        input_output_aliases={0: 0},
        compiler_params=params(),
    )(v, *tokens)


def sum_y(v, core):
    v = v + swap(v)
    a = lax.ppermute(v, F, plane_moves(lambda z, y, c: (z, y ^ (1 + c), c)))
    b = lax.ppermute(v, F, plane_moves(lambda z, y, c: (z, y ^ 3, c) if c else None))
    q = jnp.where(core == 0, v + a, a + b)
    return q, swap(q)


def on_device(
    inputs,
    norm_gain_vector,
    weight,
    down_adapters,
    up_adapters,
    tenant,
    tenant_slot_index,
    live_row_count,
    cotangent,
    down_row_factor,
    down_column_factor,
    up_row_factor,
    up_column_factor,
):
    dp = lax.axis_index("dp")
    z, y, core = lax.axis_index("z"), lax.axis_index("y"), lax.axis_index("core")
    opposite = 1 - core
    sign = 1 - 2 * core
    y_two, y_keep, y_send = (y + 2) % NY, (y + 1 + 2 * core) % NY, (y + 3 + 2 * core) % NY
    z_steps = [(z + NZ - s * sign * way) % NZ for s in (1, 2, 3) for way in (1, -1)]
    z_far = (z + NZ // 2) % NZ
    spots = jnp.stack(
        [y_two, opposite, y_send, core, y_send, opposite, y, opposite]
        + [y_two, core, y_keep, opposite, y_keep, core, y, core]
        + [z, y, core, dp]
        + z_steps
        + [z_far]
    ).astype(i32)
    down = down_adapters.transpose(1, 2, 0).reshape(TENANTS * RANK, WIDTH)
    up = up_adapters.reshape(TENANTS * RANK, WIDTH)
    tenant = tenant.reshape(1, ROWS)
    w5 = weight.reshape(NZ, NY, NC, WIDTH, WIDTH)
    w4 = weight.reshape(NZ, NY * NC, WIDTH, WIDTH)

    message, both, turned = rows_kernel(
        live_row_count, inputs, norm_gain_vector, cotangent, down, up, tenant
    )
    s_two, s_far = part_kernel(w5, turned, spots, 0, [[], []], [])
    own = [message] + [lax.ppermute(message, "y", turn(NY, k)) for k in (3, 2, 1)]
    own[1] = tied(own[1], s_two)
    other = [swap(v) for v in own]
    boths = lax.all_to_all(both, "dp", 0, 0, tiled=True)

    block = block_kernel(spots, own, other)
    s_near, s_own = part_kernel(w5, turned, spots, 2, [[], []], [block])
    r_two, r_far, r_near, r_own = [swap(v) for v in (s_two, s_far, s_near, s_own)]
    t_two, t_far = part_kernel(w5, turned, spots, 4, [[r_two], [r_far]], [block])
    g_two = lax.ppermute(t_two, F, Y_BY_CORE)
    g_far = lax.ppermute(t_far, F, Y_BY_CORE)
    frozen_zero = frozen_kernel(w4, spots, None, [block], [16])

    one = tied(lax.ppermute(block, F, Z_BY_CORE), t_far, s_near)
    one_o = swap(one)
    two = lax.ppermute(one, F, Z_BY_CORE)
    (t_near,) = part_kernel(w5, turned, spots, 6, [[r_near, g_two]], [])
    g_near = lax.ppermute(t_near, F, Y_BY_CORE)
    two = tied(two, g_two, frozen_zero)
    two_o = swap(two)
    frozen_one = frozen_kernel(w4, spots, frozen_zero, [one, one_o], [20, 21])
    three = lax.ppermute(two, F, Z_BY_CORE)
    three = tied(three, t_near, frozen_one)
    three_o = swap(three)
    frozen_two = frozen_kernel(w4, spots, frozen_one, [two, two_o], [22, 23])
    four = lax.ppermute(three, F, Z_BY_CORE)
    frozen_three = frozen_kernel(w4, spots, frozen_two, [three, three_o], [24, 25])
    four = tied(four, frozen_three, boths)

    small, back, scale = small_kernel(
        spots, [block, one, one_o, two, two_o, three, three_o, four], tenant
    )
    smalls = lax.all_to_all(small, "dp", 0, 0, tiled=True)
    projected = final_kernel(w4, spots, frozen_three, four, 26, scale, small, up, tenant)
    ga, gb, row_a_new, col_b_new, moments = slots_kernel(
        tenant_slot_index,
        spots,
        smalls,
        boths,
        down_row_factor,
        up_column_factor,
        projected,
    )
    moments = sum_y(moments, core)

    adds = [r_own, swap(g_far), g_near]
    reduced = last_part_kernel(w5, turned, spots, 7, ORDER, adds, moments, [])
    pieces = [reduced[0]]
    for k, piece in zip(ORDER[1:], reduced[1:]):
        pieces.append(lax.ppermute(piece, "z", turn(NZ, k)))
    normed_gradient_transposed = gradient_kernel(pieces, down, back, tenant)
    update_a, update_b, col_a_new, row_b_new = update_kernel(
        spots,
        pieces,
        ga,
        gb,
        row_a_new,
        col_b_new,
        down_column_factor,
        up_row_factor,
    )
    return (
        projected,
        normed_gradient_transposed,
        update_a.reshape(OWNED, RANK, WIDTH).swapaxes(1, 2),
        update_b.reshape(OWNED, RANK, WIDTH),
        row_a_new,
        col_a_new,
        row_b_new,
        col_b_new,
    )


def solution(mesh):
    split = Mesh(mesh.devices.reshape(NX, NZ, NY, NC), ("dp",) + F)
    return jax.shard_map(
        on_device,
        mesh=split,
        in_specs=(
            P("dp", F),
            P(F),
            P(None, F),
            P(F, None, None),
            P(None, None, F),
            P("dp"),
            P(),
            P("dp"),
            P("dp", F),
            P("dp", F),
            P("dp", None),
            P("dp", None),
            P("dp", F),
        ),
        out_specs=(
            P("dp", F),
            P(F, "dp"),
            P("dp", F, None),
            P("dp", None, F),
            P("dp", F),
            P("dp", None),
            P("dp", None),
            P("dp", F),
        ),
        check_vma=False,
    )
```

```python
import functools

import jax
import jax.numpy as jnp
from jax import lax
from jax.experimental import pallas as pl
from jax.experimental.pallas import tpu as pltpu
from jax.sharding import Mesh, PartitionSpec as P

ADAPTER_SCALE = 0.5
BETA_TWO = 0.9
SQ_EPS = 1e-30
RMS_EPS = 1e-05
NX, NZ, NY, NC = 4, 8, 4, 2
F = ("z", "y", "core")
bf16, f32, i32 = jnp.bfloat16, jnp.float32, jnp.int32
NT = (((1,), (1,)), ((), ()))
NN = (((1,), (0,)), ((), ()))
TN = (((0,), (0,)), ((), ()))
ROWS, WIDTH, FULL, TENANTS, RANK, OWNED = 128, 256, 16384, 16, 32, 8
HBM = pl.BlockSpec(memory_space=pl.ANY)
VMEM = pl.BlockSpec(memory_space=pltpu.VMEM)
SMEM = pl.BlockSpec(memory_space=pltpu.SMEM)


def plane_moves(rule):
    pairs = []
    for z in range(NZ):
        for y in range(NY):
            for c in range(NC):
                to = rule(z, y, c)
                if to is not None:
                    z2, y2, c2 = to
                    pairs.append(
                        ((z * NY + y) * NC + c, ((z2 % NZ) * NY + y2 % NY) * NC + c2)
                    )
    return pairs


Z_BY_CORE = plane_moves(lambda z, y, c: (z + 1 - 2 * c, y, c))
Y_BY_CORE = plane_moves(lambda z, y, c: (z, y + 1 - 2 * c, c))


def turn(n, k):
    return [(i, (i + k) % n) for i in range(n)]


def swap(v):
    return lax.ppermute(v, "core", turn(NC, 1))


def like(shape, dtype):
    return jax.ShapeDtypeStruct(shape, dtype)


def tile_of(v):
    return pl.BlockSpec(v.shape, lambda *_, n=v.ndim: (0,) * n)


def whole(shape):
    return pl.BlockSpec(shape, lambda *_, n=len(shape): (0,) * n)


def params(n=48):
    return pltpu.CompilerParams(vmem_limit_bytes=n * 1024 * 1024)


def cost(flops, moved):
    return pl.CostEstimate(flops=flops, bytes_accessed=moved, transcendentals=0)


def dot(a, b, dims=NN):
    return lax.dot_general(a, b, dims, preferred_element_type=f32)


def column_to_rows(v):
    return jnp.broadcast_to(v, (v.shape[0], 128)).T


def row_to_columns(v):
    return jnp.broadcast_to(v, (128, v.shape[1])).T


def split_store(ref, at, v):
    n = v.shape[0]
    high = v.astype(bf16)
    ref[at : at + n] = high
    ref[at + n : at + 2 * n] = (v - high.astype(f32)).astype(bf16)


def split_load(ref, at, n):
    return ref[at : at + n].astype(f32) + ref[at + n : at + 2 * n].astype(f32)


PACKED = 2 * RANK + 16
MESSAGE = 2 * ROWS + 2 * PACKED


def rows_body(live_ref, x_ref, gain_ref, cot_ref, down_ref, up_ref, tenant_ref, message_ref, both_ref, turned_ref):
    x = x_ref[...].astype(f32)
    gained = (x * gain_ref[...].astype(f32)[None, :]).astype(bf16)
    at = lax.broadcasted_iota(i32, (ROWS, WIDTH), 0)
    grad = jnp.where(at < live_ref[0], cot_ref[...].astype(f32), 0.0)
    turned_ref[...] = grad.T.astype(bf16)
    grad = grad.astype(bf16)
    for k in range(NX):
        both_ref[k, 0] = gained
        both_ref[k, 1] = grad
    message_ref[:ROWS] = gained[:, :128]
    message_ref[ROWS : 2 * ROWS] = gained[:, 128:]
    tenant = tenant_ref[...]
    parts = []
    for w_ref, v in ((down_ref, gained), (up_ref, grad)):
        every = dot(w_ref[...], v, NT)
        picked = jnp.zeros((RANK, ROWS), f32)
        for t in range(TENANTS):
            picked = picked + jnp.where(tenant == t, every[t * RANK : (t + 1) * RANK], 0.0)
        parts.append(picked)
    parts.append(column_to_rows(jnp.sum(x * x, axis=1, keepdims=True))[:16])
    split_store(message_ref, 2 * ROWS, jnp.concatenate(parts))


def rows_kernel(live, x, gain, cot, down, up, tenant):
    return pl.pallas_call(
        rows_body,
        grid=(1,),
        in_specs=[SMEM] + [tile_of(v) for v in (x, gain, cot, down, up, tenant)],
        out_specs=[whole((MESSAGE, 128)), whole((NX, 2, ROWS, WIDTH)), whole((WIDTH, ROWS))],
        out_shape=[
            like((MESSAGE, 128), bf16),
            like((NX, 2, ROWS, WIDTH), bf16),
            like((WIDTH, ROWS), bf16),
        ],
        compiler_params=params(60),
        cost_estimate=cost(2**26, 2**20),
    )(live, x, gain, cot, down, up, tenant)


def part_body(counts, spots_ref, turned_ref, *refs):
    n = len(counts)
    refs = list(refs)
    w = [refs.pop(0) for _ in range(n)]
    adds = [[refs.pop(0) for _ in range(k)] for k in counts]
    outs = refs[len(refs) - n :]
    turned = turned_ref[...]
    for i in range(n):
        many = w[i].shape[0]
        total = dot(w[i][...].reshape(many * WIDTH, WIDTH), turned)
        for a in adds[i]:
            total = total + a[...].reshape(many * WIDTH, ROWS).astype(f32)
        outs[i][...] = total.astype(bf16).reshape(many, WIDTH, ROWS)


def part_kernel(w5, turned, spots, first, adds, tokens, tiles=2):
    n = len(adds)
    step = NZ // tiles
    w_specs = [
        pl.BlockSpec(
            (step, 1, 1, WIDTH, WIDTH),
            lambda i, s, k=k: (i, s[2 * (first + k)], s[2 * (first + k) + 1], 0, 0),
        )
        for k in range(n)
    ]
    tile = pl.BlockSpec((step, WIDTH, ROWS), lambda i, s: (i, 0, 0))
    flat = [a for some in adds for a in some]
    return pl.pallas_call(
        functools.partial(part_body, [len(a) for a in adds]),
        grid_spec=pltpu.PrefetchScalarGridSpec(
            num_scalar_prefetch=1,
            grid=(tiles,),
            in_specs=[pl.BlockSpec((WIDTH, ROWS), lambda i, s: (0, 0))]
            + w_specs
            + [tile] * len(flat)
            + [HBM] * len(tokens),
            out_specs=[tile] * n,
        ),
        out_shape=[like((NZ, WIDTH, ROWS), bf16)] * n,
        compiler_params=params(),
        cost_estimate=cost(n * 2**27, n * 2**21),
    )(spots, turned, *([w5] * n), *flat, *tokens)


MOMENTS = 2 * 8
PIECE = WIDTH + 2 * MOMENTS
ORDER = (0, 4, 3, 5, 2, 6, 1, 7)


def last_part_body(offsets, spots_ref, turned_ref, w_ref, a_ref, b_ref, c_ref, p_ref, q_ref, *refs):
    outs = refs[len(refs) - len(offsets) :]
    z = spots_ref[16]
    moments = p_ref[...] + q_ref[...]
    moments = jnp.concatenate([moments[:, :128], moments[:, 128:]])
    for k, out in zip(offsets, outs):
        at = (z + k) % NZ
        t = dot(w_ref[at, 0, 0], turned_ref[...])
        for a in (a_ref, b_ref, c_ref):
            t = t + a[at].astype(f32)
        out[:WIDTH] = t.astype(bf16)
        split_store(out, WIDTH, moments)


def last_part_kernel(w5, turned, spots, at, offsets, adds, moments, tokens):
    flat = pl.BlockSpec((WIDTH, ROWS), lambda i, s: (0, 0))
    wide = pl.BlockSpec((8, OWNED * RANK), lambda i, s: (0, 0))
    out = pl.BlockSpec((PIECE, ROWS), lambda i, s: (0, 0))
    return pl.pallas_call(
        functools.partial(last_part_body, offsets),
        grid_spec=pltpu.PrefetchScalarGridSpec(
            num_scalar_prefetch=1,
            grid=(1,),
            in_specs=[
                flat,
                pl.BlockSpec(
                    (NZ, 1, 1, WIDTH, WIDTH), lambda i, s: (0, s[2 * at], s[2 * at + 1], 0, 0)
                ),
            ]
            + [whole((NZ, WIDTH, ROWS))] * 3
            + [wide] * 2
            + [HBM] * len(tokens),
            out_specs=[out] * len(offsets),
        ),
        out_shape=[like((PIECE, ROWS), bf16)] * len(offsets),
        compiler_params=params(),
        cost_estimate=cost(2**27, 2**21),
    )(spots, turned, w5, *adds, *moments, *tokens)


BLOCK = NY * NC * 2 * ROWS
TAIL = 2 * ROWS


def block_body(spots_ref, *refs):
    own, other = refs[:NY], refs[NY : 2 * NY]
    block_ref, parts_ref = refs[-2:]
    y, core = spots_ref[17], spots_ref[18]
    for j in range(NY):
        at = ((y + j) % NY) * NC
        for spot, ref in ((at + core, own[j]), (at + 1 - core, other[j])):
            block_ref[pl.ds(pl.multiple_of(spot * 2 * ROWS, 2 * ROWS), 2 * ROWS)] = ref[
                : 2 * ROWS
            ]
            parts_ref[spot] = split_load(ref, 2 * ROWS, PACKED)
    total = parts_ref[0]
    for k in range(1, NY * NC):
        total = total + parts_ref[k]
    split_store(block_ref, BLOCK, total)
    block_ref[BLOCK + 2 * PACKED :] = jnp.zeros((TAIL - 2 * PACKED, 128), bf16)


def block_kernel(spots, own, other, *tokens):
    return pl.pallas_call(
        block_body,
        in_specs=[SMEM] + [VMEM] * (2 * NY) + [HBM] * len(tokens),
        out_specs=VMEM,
        out_shape=like((BLOCK + TAIL, 128), bf16),
        scratch_shapes=[pltpu.VMEM((NY * NC, PACKED, ROWS), f32)],
        compiler_params=params(),
    )(spots, *own, *other, *tokens)


def long_dot(x_ref, w_ref):
    many = x_ref.shape[0] // ROWS
    x = jnp.concatenate([x_ref[g * ROWS : (g + 1) * ROWS] for g in range(many)], axis=1)
    return dot(x, w_ref[...].reshape(many * 128, WIDTH))


def frozen_body(n, has_acc, spots_ref, *refs):
    refs = list(refs)
    acc_ref = refs.pop(0) if has_acc else None
    xs, ws, out_ref = refs[:n], refs[n : 2 * n], refs[-1]
    total = None
    for x_ref, w_ref in zip(xs, ws):
        term = long_dot(x_ref, w_ref)
        total = term if total is None else total + term

    @pl.when(pl.program_id(0) == 0)
    def _():
        out_ref[...] = total + acc_ref[...] if has_acc else total

    @pl.when(pl.program_id(0) > 0)
    def _():
        out_ref[...] = out_ref[...] + total


def frozen_kernel(w4, spots, acc, blocks, ats, tokens=(), tiles=2):
    n = len(blocks)
    flat = pl.BlockSpec((ROWS, WIDTH), lambda i, s: (0, 0))
    step = NY * NC // tiles
    has_acc = acc is not None
    return pl.pallas_call(
        functools.partial(frozen_body, n, has_acc),
        grid_spec=pltpu.PrefetchScalarGridSpec(
            num_scalar_prefetch=1,
            grid=(tiles,),
            in_specs=[flat] * has_acc
            + [pl.BlockSpec((step * 2 * ROWS, 128), lambda i, s: (i, 0))] * n
            + [
                pl.BlockSpec((1, step, WIDTH, WIDTH), lambda i, s, a=a: (s[a], i, 0, 0))
                for a in ats
            ]
            + [HBM] * len(tokens),
            out_specs=flat,
        ),
        out_shape=like((ROWS, WIDTH), f32),
        compiler_params=params(),
        cost_estimate=cost(n * 2**27, 9 * 2**20),
    )(spots, *([acc] * has_acc), *blocks, *([w4] * n), *tokens)


def final_body(spots_ref, acc_ref, x_ref, w_ref, scale_ref, small_ref, up_ref, tenant_ref, out_ref):
    total = acc_ref[...] + long_dot(x_ref, w_ref)
    tenant = tenant_ref[...]
    inner = small_ref[0, :RANK].astype(f32)
    spread = jnp.concatenate([jnp.where(tenant == t, inner, 0.0) for t in range(TENANTS)])
    adapted = dot(spread.T.astype(bf16), up_ref[...])
    scale = row_to_columns(scale_ref[:1])[:, :1]
    out_ref[...] = (scale * total + ADAPTER_SCALE * adapted).astype(bf16)


def final_kernel(w4, spots, acc, x, at, scale, small, up, tenant):
    def full(v):
        return pl.BlockSpec(v.shape, lambda i, s, n=v.ndim: (0,) * n)

    return pl.pallas_call(
        final_body,
        grid_spec=pltpu.PrefetchScalarGridSpec(
            num_scalar_prefetch=1,
            grid=(1,),
            in_specs=[
                full(acc),
                pl.BlockSpec((BLOCK, 128), lambda i, s: (0, 0)),
                pl.BlockSpec((1, NY * NC, WIDTH, WIDTH), lambda i, s: (s[at], 0, 0, 0)),
            ]
            + [full(v) for v in (scale, small, up, tenant)],
            out_specs=full(acc),
        ),
        out_shape=like((ROWS, WIDTH), bf16),
        compiler_params=params(),
        cost_estimate=cost(2**28, 9 * 2**20),
    )(spots, acc, x, w4, scale, small, up, tenant)


def gradient_body(*refs):
    pieces, (down_ref, back_ref, tenant_ref), out_ref = refs[:NZ], refs[NZ : NZ + 3], refs[-1]
    total = pieces[0][:WIDTH].astype(f32)
    for p in pieces[1:]:
        total = total + p[:WIDTH].astype(f32)
    tenant = tenant_ref[...]
    back = back_ref[...].astype(f32)
    spread = jnp.concatenate([jnp.where(tenant == t, back, 0.0) for t in range(TENANTS)])
    adapter = dot(down_ref[...].astype(f32).T.astype(bf16), spread.astype(bf16))
    out_ref[...] = (total + ADAPTER_SCALE * adapter).astype(bf16)


def gradient_kernel(pieces, down, back, tenant, *tokens):
    return pl.pallas_call(
        gradient_body,
        grid=(1,),
        in_specs=[VMEM] * NZ + [tile_of(v) for v in (down, back, tenant)] + [HBM] * len(tokens),
        out_specs=VMEM,
        out_shape=like((WIDTH, ROWS), bf16),
        compiler_params=params(),
        cost_estimate=cost(2**25, 2**20),
    )(*pieces, down, back, tenant, *tokens)


def small_body(spots_ref, *refs):
    parts, tenant_ref = refs[:NZ], refs[NZ]
    small_ref, back_ref, scale_ref, all_ref = refs[-4:]
    for at, ref in zip((16, 20, 21, 22, 23, 24, 25, 26), parts):
        all_ref[spots_ref[at]] = split_load(ref, 0, PACKED)
    total = all_ref[0]
    for k in range(1, NZ):
        total = total + all_ref[k]
    scale = lax.rsqrt(total[2 * RANK : 2 * RANK + 1] / FULL + RMS_EPS)
    back = total[RANK : 2 * RANK]
    for k in range(NX):
        small_ref[k, :RANK] = (total[:RANK] * scale).astype(bf16)
        small_ref[k, RANK : 2 * RANK] = (back * scale).astype(bf16)
        small_ref[k, 2 * RANK :] = jnp.broadcast_to(
            tenant_ref[...].astype(f32), (16, ROWS)
        ).astype(bf16)
    back_ref[...] = back.astype(bf16)
    scale_ref[...] = jnp.broadcast_to(scale, (8, ROWS))


def small_kernel(spots, blocks, tenant, *tokens):
    return pl.pallas_call(
        small_body,
        grid=(1,),
        in_specs=[SMEM]
        + [pl.BlockSpec((TAIL, 128), lambda i: (BLOCK // TAIL, 0))] * NZ
        + [tile_of(tenant)]
        + [HBM] * len(tokens),
        out_specs=[whole((NX, 2 * RANK + 16, ROWS)), whole((RANK, ROWS)), whole((8, ROWS))],
        out_shape=[
            like((NX, 2 * RANK + 16, ROWS), bf16),
            like((RANK, ROWS), bf16),
            like((8, ROWS), f32),
        ],
        scratch_shapes=[pltpu.VMEM((NZ, PACKED, ROWS), f32)],
        compiler_params=params(),
    )(spots, *blocks, tenant, *tokens)


def lift(v, size):
    return jnp.broadcast_to(v[:, None, :], (OWNED, RANK, size)).reshape(OWNED * RANK, size)


def slots_body(slot_ref, spots_ref, *refs):
    smalls, boths, row_ref, col_ref = refs[:4]
    ga_ref, gb_ref, row_out, col_out, sum_ref = refs[-5:]
    first = spots_ref[19] * OWNED
    a_rows, b_rows = [], []
    for k in range(NX):
        small_ref = smalls.at[k]
        tenant = small_ref[2 * RANK : 2 * RANK + 16].astype(f32)[:1]
        slot = jnp.full((1, ROWS), -1, i32)
        for t in range(TENANTS):
            slot = jnp.where(tenant == t, slot_ref[t], slot)
        inner = small_ref[:RANK].astype(f32)
        back = small_ref[RANK : 2 * RANK].astype(f32)
        a_rows.append(
            jnp.concatenate([jnp.where(slot == first + s, back, 0.0) for s in range(OWNED)])
        )
        b_rows.append(
            jnp.concatenate([jnp.where(slot == first + s, inner, 0.0) for s in range(OWNED)])
        )
    for rows, at, out_ref in ((a_rows, 0, ga_ref), (b_rows, 1, gb_ref)):
        total = dot(rows[0].astype(bf16), boths[0, at])
        for k in range(1, NX):
            total = total + dot(rows[k].astype(bf16), boths[k, at])
        out_ref[...] = ADAPTER_SCALE * total
    sq_a = ga_ref[...] * ga_ref[...] + SQ_EPS
    sq_b = gb_ref[...] * gb_ref[...] + SQ_EPS
    row_new = BETA_TWO * row_ref[...] + (1.0 - BETA_TWO) * (
        jnp.sum(sq_a.reshape(OWNED, RANK, WIDTH), axis=1) / RANK
    )
    row_out[...] = row_new
    col_out[...] = BETA_TWO * col_ref[...] + (1.0 - BETA_TWO) * (
        jnp.sum(sq_b.reshape(OWNED, RANK, WIDTH), axis=1) / RANK
    )
    lane = lax.broadcasted_iota(i32, (OWNED * RANK, 128), 1)
    columns = [jnp.sum(v, axis=1, keepdims=True) for v in (sq_a, sq_b, lift(row_new, WIDTH))]
    mixed = jnp.where(lane == 0, columns[0], jnp.where(lane == 1, columns[1], columns[2]))
    sum_ref[...] = mixed.T[:8]


def slots_kernel(slot, spots, smalls, boths, row, col, *tokens):
    n = OWNED * RANK
    return pl.pallas_call(
        slots_body,
        grid=(1,),
        in_specs=[SMEM] * 2
        + [tile_of(v) for v in (smalls, boths, row, col)]
        + [HBM] * len(tokens),
        out_specs=[whole((n, WIDTH))] * 2 + [whole((OWNED, WIDTH))] * 2 + [whole((8, n))],
        out_shape=[like((n, WIDTH), f32)] * 2
        + [like((OWNED, WIDTH), f32)] * 2
        + [like((8, n), f32)],
        compiler_params=params(60),
        cost_estimate=cost(2**27, 2**21),
    )(slot, spots, smalls, boths, row, col, *tokens)


def update_body(spots_ref, *refs):
    pieces = refs[:NZ]
    ga_ref, gb_ref, row_ref, col_ref, dcol_ref, urow_ref = refs[NZ : NZ + 6]
    ua_ref, ub_ref, ca_ref, rb_ref, parts_ref = refs[NZ + 6 :]
    z = spots_ref[16]
    for k, ref in zip(ORDER, pieces):
        parts_ref[(z + NZ - k) % NZ] = split_load(ref, WIDTH, MOMENTS)
    total = parts_ref[0]
    for k in range(1, NZ):
        total = total + parts_ref[k]
    total = jnp.concatenate([total[:8], total[8:]], axis=1)
    total = jnp.concatenate([total, jnp.zeros((120, 2 * ROWS), f32)]).T
    same = lax.broadcasted_iota(i32, (OWNED, RANK, RANK), 1) == lax.broadcasted_iota(
        i32, (OWNED, RANK, RANK), 2
    )

    def mixed(old_ref, sums, out_ref):
        old = jnp.where(same, old_ref[...][:, None, :], 0.0)
        old = jnp.sum(old, axis=2, keepdims=True).reshape(OWNED * RANK, 1)
        new = BETA_TWO * old + (1.0 - BETA_TWO) * (sums / FULL)
        back = jnp.broadcast_to(new, (OWNED * RANK, RANK)).reshape(OWNED, RANK, RANK)
        out_ref[...] = jnp.sum(jnp.where(same, back, 0.0), axis=1)
        return new

    col_a = mixed(dcol_ref, total[:, 0:1], ca_ref)
    row_b = mixed(urow_ref, total[:, 1:2], rb_ref)
    mean_a = total[:, 2:3] / FULL
    wide = jnp.broadcast_to(row_b, (OWNED * RANK, 128)).reshape(OWNED, RANK, 128)
    mean_b = lift(jnp.sum(wide, axis=1), 128)[:, :1] / RANK
    ua_ref[...] = ga_ref[...] * lax.rsqrt(lift(row_ref[...], WIDTH) * col_a / mean_a)
    ub_ref[...] = gb_ref[...] * lax.rsqrt(row_b * lift(col_ref[...], WIDTH) / mean_b)


def update_kernel(spots, pieces, ga, gb, row, col, dcol, urow):
    n = OWNED * RANK
    return pl.pallas_call(
        update_body,
        grid=(1,),
        in_specs=[SMEM] + [VMEM] * NZ + [tile_of(v) for v in (ga, gb, row, col, dcol, urow)],
        out_specs=[VMEM] * 4,
        out_shape=[like((n, WIDTH), f32)] * 2 + [like((OWNED, RANK), f32)] * 2,
        scratch_shapes=[pltpu.VMEM((NZ, MOMENTS, 128), f32)],
        compiler_params=params(),
        cost_estimate=cost(2**20, 2**20),
    )(spots, *pieces, ga, gb, row, col, dcol, urow)


def tied_body(*refs):
    pass


def tied(v, *tokens):
    return pl.pallas_call(
        tied_body,
        in_specs=[HBM] * (1 + len(tokens)),
        out_specs=HBM,
        out_shape=like(v.shape, v.dtype),
        input_output_aliases={0: 0},
        compiler_params=params(),
    )(v, *tokens)


def sum_y(v, core):
    v = v + swap(v)
    a = lax.ppermute(v, F, plane_moves(lambda z, y, c: (z, y ^ (1 + c), c)))
    b = lax.ppermute(v, F, plane_moves(lambda z, y, c: (z, y ^ 3, c) if c else None))
    q = jnp.where(core == 0, v + a, a + b)
    return q, swap(q)


def on_device(
    inputs,
    norm_gain_vector,
    weight,
    down_adapters,
    up_adapters,
    tenant,
    tenant_slot_index,
    live_row_count,
    cotangent,
    down_row_factor,
    down_column_factor,
    up_row_factor,
    up_column_factor,
):
    dp = lax.axis_index("dp")
    z, y, core = lax.axis_index("z"), lax.axis_index("y"), lax.axis_index("core")
    opposite = 1 - core
    sign = 1 - 2 * core
    y_two, y_keep, y_send = (y + 2) % NY, (y + 1 + 2 * core) % NY, (y + 3 + 2 * core) % NY
    z_steps = [(z + NZ - s * sign * way) % NZ for s in (1, 2, 3) for way in (1, -1)]
    z_far = (z + NZ // 2) % NZ
    spots = jnp.stack(
        [y_two, opposite, y_send, core, y_send, opposite, y, opposite]
        + [y_two, core, y_keep, opposite, y_keep, core, y, core]
        + [z, y, core, dp]
        + z_steps
        + [z_far]
    ).astype(i32)
    down = down_adapters.transpose(1, 2, 0).reshape(TENANTS * RANK, WIDTH)
    up = up_adapters.reshape(TENANTS * RANK, WIDTH)
    tenant = tenant.reshape(1, ROWS)
    w5 = weight.reshape(NZ, NY, NC, WIDTH, WIDTH)
    w4 = weight.reshape(NZ, NY * NC, WIDTH, WIDTH)

    message, both, turned = rows_kernel(
        live_row_count, inputs, norm_gain_vector, cotangent, down, up, tenant
    )
    s_two, s_far = part_kernel(w5, turned, spots, 0, [[], []], [])
    own = [message] + [lax.ppermute(message, "y", turn(NY, k)) for k in (3, 2, 1)]
    own[1] = tied(own[1], s_two)
    other = [swap(v) for v in own]
    boths = lax.all_to_all(both, "dp", 0, 0, tiled=True)

    block = block_kernel(spots, own, other)
    s_near, s_own = part_kernel(w5, turned, spots, 2, [[], []], [block])
    r_two, r_far, r_near, r_own = [swap(v) for v in (s_two, s_far, s_near, s_own)]
    t_two, t_far = part_kernel(w5, turned, spots, 4, [[r_two], [r_far]], [block])
    g_two = lax.ppermute(t_two, F, Y_BY_CORE)
    g_far = lax.ppermute(t_far, F, Y_BY_CORE)
    frozen_zero = frozen_kernel(w4, spots, None, [block], [16])

    one = tied(lax.ppermute(block, F, Z_BY_CORE), t_far, s_near)
    one_o = swap(one)
    two = lax.ppermute(one, F, Z_BY_CORE)
    (t_near,) = part_kernel(w5, turned, spots, 6, [[r_near, g_two]], [])
    g_near = lax.ppermute(t_near, F, Y_BY_CORE)
    two = tied(two, t_near, frozen_zero)
    two_o = swap(two)
    frozen_one = frozen_kernel(w4, spots, frozen_zero, [one, one_o], [20, 21])
    three = lax.ppermute(two, F, Z_BY_CORE)
    three = tied(three, frozen_one, boths)
    three_o = swap(three)
    frozen_two = frozen_kernel(w4, spots, frozen_one, [two, two_o], [22, 23])
    four = lax.ppermute(three, F, Z_BY_CORE)
    frozen_three = frozen_kernel(w4, spots, frozen_two, [three, three_o], [24, 25])
    four = tied(four, frozen_three)

    small, back, scale = small_kernel(
        spots, [block, one, one_o, two, two_o, three, three_o, four], tenant
    )
    smalls = lax.all_to_all(small, "dp", 0, 0, tiled=True)
    projected = final_kernel(w4, spots, frozen_three, four, 26, scale, small, up, tenant)
    ga, gb, row_a_new, col_b_new, moments = slots_kernel(
        tenant_slot_index,
        spots,
        smalls,
        boths,
        down_row_factor,
        up_column_factor,
        projected,
    )
    moments = sum_y(moments, core)

    adds = [r_own, swap(g_far), g_near]
    reduced = last_part_kernel(w5, turned, spots, 7, ORDER, adds, moments, [])
    pieces = [reduced[0]]
    for k, piece in zip(ORDER[1:], reduced[1:]):
        pieces.append(lax.ppermute(piece, "z", turn(NZ, k)))
    normed_gradient_transposed = gradient_kernel(pieces, down, back, tenant)
    update_a, update_b, col_a_new, row_b_new = update_kernel(
        spots,
        pieces,
        ga,
        gb,
        row_a_new,
        col_b_new,
        down_column_factor,
        up_row_factor,
    )
    return (
        projected,
        normed_gradient_transposed,
        update_a.reshape(OWNED, RANK, WIDTH).swapaxes(1, 2),
        update_b.reshape(OWNED, RANK, WIDTH),
        row_a_new,
        col_a_new,
        row_b_new,
        col_b_new,
    )


def solution(mesh):
    split = Mesh(mesh.devices.reshape(NX, NZ, NY, NC), ("dp",) + F)
    return jax.shard_map(
        on_device,
        mesh=split,
        in_specs=(
            P("dp", F),
            P(F),
            P(None, F),
            P(F, None, None),
            P(None, None, F),
            P("dp"),
            P(),
            P("dp"),
            P("dp", F),
            P("dp", F),
            P("dp", None),
            P("dp", None),
            P("dp", F),
        ),
        out_specs=(
            P("dp", F),
            P(F, "dp"),
            P("dp", F, None),
            P("dp", None, F),
            P("dp", F),
            P("dp", None),
            P("dp", None),
            P("dp", F),
        ),
        check_vma=False,
    )
```
